256 devices in a mesh: dp: 16 (over y, x), seq: 16 (over z, core).
Axes of the slice: x: 4, y: 4, z: 8, core: 2. Of those that a mesh axis runs over, the one named last changes fastest.
Arguments:
- loaded: float32 [16, 96, 1664], P('seq', 'dp'), may hold values from -24 to 24
- tile_rows: int32 [16, 96], P('seq', 'dp'), may hold values from 0 to 95, as said below
- bucket_ids: int32 [4], replicated, may hold values from 0 to 3, as said below
- in_weight: float32 [96, 81], replicated, may hold values from -0.625 to 0.625
- in_bias: float32 [96], replicated, may hold values from -3 to 3
- bucket_bias: float32 [4, 96], replicated, may hold values from -4 to 4
- norm_gain: float32 [96], replicated, may hold values from 0.5 to 1.5
- mid_weight: float32 [27, 96, 96], replicated, may hold values from -0.125 to 0.125
- mid_bias: float32 [96], replicated, may hold values from -3 to 3
- head_gain: float32 [96], replicated, may hold values from 0.5 to 1.5
- head_weight: float32 [16, 96], replicated, may hold values from -0.625 to 0.625
- head_bias: float32 [16], replicated, may hold values from -3 to 3
Outputs:
- latent_tokens: float32 [16, 32, 26624], P(None, 'dp', 'seq')
The draws below stay inside these ranges and needn't reach their ends.
Inputs may be any that keep to these rules, and one draw needn't show every extreme that they name: For each frame, tile_rows[g] is a permutation of the 96 tiles. The 6 entries held by one index of dp name at most 2 tiles of any one row band (band o holds tiles 6 * o to 6 * o + 5), and in every frame some index of dp names exactly 2 tiles of some band. `bucket_ids`: clips whose numbers differ by less than 4 have different buckets; clips whose numbers differ by 4 have the same one.
All inputs are finite; a program needn't handle non-finite values.
Results may differ from the reference program's by a relative error of at most 0.0003.
Values sent between devices are 32-bit elements; how exact they have to be, the bound alone decides.
A program may use at most 128 MiB of HBM per device.

```python
import math
import jax
import jax.numpy as jnp
from jax import lax

CH = 96
ZCH = 16
W = 832
ROWS_DEV = 4
FRAMES = 4
BUCKETS = 4
NF = 16
CLIPS = 4
H = 64
TILES_DEV = 6
TILES_ALL = 96
N_DP = 16


def draw_loaded(key, part):
    key = jax.random.fold_in(key, 11)
    key_unit, key_tile, key_column = jax.random.split(key, 3)
    dims_all = (NF, TILES_ALL, 2 * W)
    unit_values = jnp.clip(jax.random.normal(key_unit, dims_all, jnp.float32), -4.0, 4.0)
    tile_scale = jnp.exp(jax.random.uniform(key_tile, (NF, TILES_ALL, 1), jnp.float32, math.log(0.3), math.log(3.0)))
    column_scale = jnp.exp(jax.random.uniform(key_column, (1, 1, 2 * W), jnp.float32, math.log(0.5), math.log(2.0)))
    return unit_values * tile_scale * column_scale


def draw_tile_rows(key, part):
    key = jax.random.fold_in(key, 23)

    def one_frame(frame_key):
        key_shift, key_owner, key_slot, key_order = jax.random.split(frame_key, 4)
        shifts = jax.random.permutation(key_shift, N_DP)
        owner_perm = jax.random.permutation(key_owner, N_DP)
        slot_perm = jax.random.permutation(key_slot, TILES_DEV)
        loaders = jnp.arange(N_DP, dtype=jnp.int32)[:, None]
        items = jnp.arange(TILES_DEV, dtype=jnp.int32)[None, :]
        classes = items // 2 % N_DP
        owners = owner_perm[(loaders + shifts[classes]) % N_DP]
        position = owners * TILES_DEV + slot_perm[items]
        orders = jax.vmap(lambda order_key: jax.random.permutation(order_key, TILES_DEV))(jax.random.split(key_order, N_DP))
        return jnp.take_along_axis(position, orders, axis=1).reshape(-1)
    return jax.vmap(one_frame)(jax.random.split(key, NF)).astype(jnp.int32)


def draw_bucket_ids(key, part):
    key = jax.random.fold_in(key, 37)
    anchor = jax.random.randint(key, (), 0, min(CLIPS, BUCKETS)).astype(jnp.int32)
    clip_nums = jnp.arange(CLIPS, dtype=jnp.int32)
    return ((BUCKETS - 1 + clip_nums - anchor + BUCKETS * CLIPS) % BUCKETS).astype(jnp.int32)


def bell_draw(stream_key, dims, width, reach, held_as=jnp.bfloat16):
    entries = width * jax.random.normal(stream_key, dims, jnp.float32)
    return jnp.clip(entries, min=-reach, max=reach).astype(held_as)


def setup_inputs(seed: int = 0) -> dict:
    key_list = jax.random.split(jax.random.key(seed), 13)
    loaded = draw_loaded(jax.random.fold_in(key_list[12], 71), 0)
    tile_rows = draw_tile_rows(jax.random.fold_in(key_list[12], 71), 0)
    bucket_ids = draw_bucket_ids(jax.random.fold_in(key_list[12], 71), 0)
    in_weight = bell_draw(key_list[3], (CH, 81), 81 ** -0.5, 0.625, jnp.float32)
    in_bias = bell_draw(key_list[4], (CH,), 0.5, 3.0, jnp.float32)
    bucket_bias = bell_draw(key_list[5], (BUCKETS, CH), 1.0, 4.0, jnp.float32)
    norm_gain = jnp.clip(1.0 + 0.1 * jax.random.normal(key_list[6], (CH,), jnp.float32), 0.5, 1.5)
    mid_weight = bell_draw(key_list[7], (27, CH, CH), (27 * CH) ** -0.5, 0.125, jnp.float32)
    mid_bias = bell_draw(key_list[8], (CH,), 0.5, 3.0, jnp.float32)
    head_gain = jnp.clip(1.0 + 0.1 * jax.random.normal(key_list[9], (CH,), jnp.float32), 0.5, 1.5)
    head_weight = bell_draw(key_list[10], (ZCH, CH), CH ** -0.5, 0.625, jnp.float32)
    head_bias = bell_draw(key_list[11], (ZCH,), 0.5, 3.0, jnp.float32)
    return dict(loaded=loaded, tile_rows=tile_rows, bucket_ids=bucket_ids, in_weight=in_weight, in_bias=in_bias, bucket_bias=bucket_bias, norm_gain=norm_gain, mid_weight=mid_weight, mid_bias=mid_bias, head_gain=head_gain, head_weight=head_weight, head_bias=head_bias)


EPSILON = 1e-06
PRECISE = lax.Precision.HIGHEST

def plane_conv(image, kernel):
    return lax.conv_general_dilated(image[None], kernel, (1, 1), ((1, 1), (1, 1)), dimension_numbers=('NCHW', 'OIHW', 'NCHW'), precision=PRECISE)[0]

def scaled_norm(values, scales):
    square = lax.optimization_barrier(jnp.mean(values * values, axis=0, keepdims=True))
    return values * lax.rsqrt(square + EPSILON) * scales[:, None, None]

def reference(loaded, tile_rows, bucket_ids, in_weight, in_bias, bucket_bias, norm_gain, mid_weight, mid_bias, head_gain, head_weight, head_bias):
    frames_all = loaded.shape[0]
    video = jax.vmap(lambda tile_data, places: jnp.zeros_like(tile_data).at[places].set(tile_data))(loaded, tile_rows)
    video = video.reshape(frames_all, N_DP, 3, ROWS_DEV // 2, 2 * W).transpose(0, 2, 1, 3, 4).reshape(frames_all, 3, H, W)
    video_front = jnp.concatenate([jnp.zeros((4,) + video.shape[1:], jnp.float32), video], 0)
    entry_kernels = in_weight.reshape(CH, 3, 3, 3, 3).transpose(1, 0, 4, 2, 3)
    middle_kernels = mid_weight.reshape(3, 3, 3, CH, CH).transpose(0, 3, 4, 1, 2)

    def first_section(frame_id):
        frame_pos = frame_id % FRAMES
        running = jnp.zeros((CH, H, W), jnp.float32)
        for step_time in range(3):
            where_at = (frame_id - 2 + step_time + 4).astype(jnp.int32)
            source = lax.dynamic_index_in_dim(video_front, where_at, 0, keepdims=False)
            source = jnp.where(frame_pos - 2 + step_time >= 0, source, 0.0)
            running = running + plane_conv(source, entry_kernels[step_time])
        clip_id = (frame_id // FRAMES).astype(jnp.int32)
        bucket_row = bucket_bias[bucket_ids[clip_id]]
        return running + (in_bias + bucket_row)[:, None, None]

    def one_frame(frame_id):
        frame_pos = frame_id % FRAMES
        sections = [first_section(frame_id - 2 + step_time) for step_time in range(3)]
        branch = jnp.zeros((CH, H, W), jnp.float32) + mid_bias[:, None, None]
        for step_time in range(3):
            active = jax.nn.silu(scaled_norm(sections[step_time], norm_gain))
            active = jnp.where(frame_pos - 2 + step_time >= 0, active, 0.0)
            branch = branch + plane_conv(active, middle_kernels[step_time])
        summed = sections[2] + branch
        latent = jax.nn.silu(scaled_norm(summed, head_gain))
        latent = jnp.einsum('zc,chw->zhw', head_weight, latent, precision=PRECISE) + head_bias[:, None, None]
        return latent.reshape(ZCH, H // 2, 2, W // 2, 2).transpose(1, 3, 0, 2, 4).reshape(H // 2, W // 2 * ZCH * 4)
    return lax.map(one_frame, jnp.arange(frames_all, dtype=jnp.int32))
```

```python
import functools

import jax
import jax.numpy as jnp
from jax import lax
from jax.experimental import pallas as pl
from jax.experimental.pallas import tpu as pltpu
from jax.sharding import PartitionSpec as P

F32, BF16, I32 = jnp.float32, jnp.bfloat16, jnp.int32
MESH = pl.DeviceIdType.MESH
EPSILON = 1e-06
CH = 96
ZCH = 16
W = 832
NF = 16
FRAMES = 4
CLIPS = 4
N_DP = 16
N_SEQ = 16
COLS = W // N_SEQ
TILE = 2 * W
LANES = 256
MID_K = 9 * CH

G43 = (
    (1 / 4, 0.0, 0.0),
    (-1 / 6, -1 / 6, -1 / 6),
    (-1 / 6, 1 / 6, -1 / 6),
    (1 / 24, 1 / 12, 1 / 6),
    (1 / 24, -1 / 12, 1 / 6),
    (0.0, 0.0, 1.0),
)


def iota(shape, dim):
    return lax.broadcasted_iota(I32, shape, dim)


def dot(a, b):
    return jnp.dot(a, b, preferred_element_type=F32)


def halves(x):
    hi = x.astype(BF16)
    return hi, (x - hi.astype(F32)).astype(BF16)


def prepare(
    ids, in_weight, in_bias, bucket_bias, norm_gain, mid_weight, mid_bias, head_gain,
    head_weight, head_bias, u, we, wb, cols, off,
):
    for a in range(3):
        for d in range(3):
            taps = [mid_weight[9 * a + 3 * b + d] for b in range(3)]
            outer, inner = taps[0] + taps[2], taps[1]
            s4 = taps[0] * (1 / 24) + taps[2] * (1 / 6)
            made = (
                taps[0] * 0.25,
                (outer + inner) * (-1 / 6),
                (inner - outer) * (1 / 6),
                s4 + inner * (1 / 12),
                s4 - inner * (1 / 12),
                taps[2],
            )
            for w in range(6):
                hi, lo = halves(made[w])
                rows = pl.ds((2 - a) * CH, CH)
                u[w, rows, pl.ds(d * CH, CH)] = hi
                u[w, rows, pl.ds((3 + d) * CH, CH)] = hi
                u[w, rows, pl.ds((6 + d) * CH, CH)] = lo
    n = iota((81, LANES), 1)
    d, part, h, m = n // 72, n % 72 // 24, n % 24 // 12, n % 12
    key = 3 * d + m % 3
    row = 2 * (m // 3) + h
    first = n < 216
    k = iota((81, LANES), 0)
    whi, wlo = halves(in_weight[...])
    for re in range(6):
        b = row - re
        legal = first & (b >= 0) & (b <= 2)
        for a in range(3):
            hit = legal & (k == 27 * a + 9 * b + key)
            e01 = jnp.where(hit & (part < 2), 1.0, 0.0).astype(BF16)
            e2 = jnp.where(hit & (part == 2), 1.0, 0.0).astype(BF16)
            got = dot(whi, e01) + dot(wlo, e2)
            we[pl.ds(re * CH, CH), pl.ds(a * LANES, LANES)] = got.astype(BF16)
    lines = jnp.concatenate(
        [in_bias[...], bucket_bias[...], norm_gain[...], mid_bias[...], head_gain[...]], axis=0
    )
    table = jnp.transpose(lines)
    cols[:, 0:8] = table
    clip = iota((CH, LANES), 1) % 64 // 16
    total = jnp.broadcast_to(table[:, 0:1], (CH, LANES))
    for c in range(CLIPS):
        mine = sum(
            table[:, 1 + b : 2 + b] * jnp.where(ids[c] == b, 1.0, 0.0) for b in range(4)
        )
        total = total + jnp.where(clip == c, mine, 0.0)
    off[...] = total
    line = iota((128, ZCH), 0)
    spread = jnp.where(line % 64 // 4 == iota((128, ZCH), 1), 1.0, 0.0)
    hhi, hlo = halves(head_weight[...])
    line = iota((128, CH), 0)
    for part, piece in enumerate((hhi, hlo)):
        wide = dot(spread.astype(BF16), piece)
        for c4 in range(4):
            for r in range(2):
                q2, s = c4 // 2, c4 % 2
                keep = (line // 64 == q2) & (line % 2 == s) & (line % 4 // 2 == r)
                at = (c4 * 2 + r) * CH
                wb[pl.ds(part * 128, 128), pl.ds(at, CH)] = jnp.where(keep, wide, 0.0).astype(BF16)
    hb = jnp.sum(spread * head_bias[...], axis=1, keepdims=True)
    cols[:, 8:9] = hb[0:CH]
    cols[0:32, 9:10] = hb[CH:128]


def exchange_kernel(
    loaded, tiles, ids, in_weight, in_bias, bucket_bias, norm_gain, mid_weight, mid_bias,
    head_gain, head_weight, head_bias,
    video, u, we, wb, cols, off,
    got, picked, sent, send1, recv1, send2, recv2, own_sem,
):
    o, g = lax.axis_index("dp"), lax.axis_index("seq")
    barrier = pltpu.get_barrier_semaphore()
    for k in range(1, 16):
        pl.semaphore_signal(barrier, 1, device_id=(lax.rem(o + k, 16), g), device_id_type=MESH)
        pl.semaphore_signal(barrier, 1, device_id=(o, lax.rem(g + k, 16)), device_id_type=MESH)

    here = pl.ds(pl.multiple_of(o * 8, 8), 8)
    lane = iota((1, TILE), 1)
    numbers = jnp.full((1, TILE), -1000.0, F32)
    for j in range(6):
        numbers = jnp.where(lane == 8 * o + j, tiles[0, j].astype(F32), numbers)
    got[here, :] = jnp.concatenate([loaded[0], numbers, jnp.zeros((1, TILE), F32)], axis=0)
    pl.semaphore_wait(barrier, 30)

    first = []
    for k in range(1, 16):
        copy = pltpu.make_async_remote_copy(
            src_ref=got.at[here],
            dst_ref=got.at[here],
            send_sem=send1.at[k],
            recv_sem=recv1.at[k],
            device_id=(lax.rem(o + k, 16), g),
            device_id_type=MESH,
        )
        copy.start()
        first.append(copy)

    prepare(
        ids, in_weight, in_bias, bucket_bias, norm_gain, mid_weight, mid_bias, head_gain,
        head_weight, head_bias, u, we, wb, cols, off,
    )

    for copy in first:
        copy.wait()

    label = got[pl.ds(6, 1), 0:128]
    for l in range(1, 16):
        label = jnp.maximum(label, got[pl.ds(8 * l + 6, 1), 0:128])
    m = iota((24, 128), 0) % 12
    pg, c = m // 3, m % 3
    wanted = 6 * o + 6 * ((pg + 1) // 2 - 1) + 2 * c + (pg + 1) % 2
    hot = jnp.where(label == wanted.astype(F32), 1.0, 0.0).astype(BF16)
    hot2 = jnp.concatenate([hot, hot], axis=1)
    picked[:, 0:128] = jnp.zeros((24, 128), F32)
    picked[:, 128 + TILE :] = jnp.zeros((24, 128), F32)
    for at in range(0, TILE, 128):
        hi, lo = halves(got[:, at : at + 128])
        picked[:, 128 + at : 256 + at] = dot(hot2, jnp.concatenate([hi, lo], axis=0))

    half = lax.rem(g // FRAMES, 2) * 64
    lane = iota((8, 128), 1) - half
    inside = (lane >= 0) & (lane < 64)
    upper = iota((8, 128), 0) < 4
    for s in range(N_SEQ):
        col = lane + (COLS * s - 4)
        keep = inside & (col >= 0) & (col < W)
        pieces = []
        for h, rows in ((0, 0), (0, 8), (1, 8), (1, 16)):
            start = 128 + h * W + COLS * s - 4
            base = start // 128 * 128
            wide = picked[rows : rows + 8, base : base + 256]
            turned = pltpu.roll(wide, lax.rem(half + 256 - (start - base), 256), 1)
            pieces.append(turned[:, 0:128])
        sent[s, 0:8] = jnp.where(keep, pieces[0], 0.0)
        sent[s, 8:16] = jnp.where(keep, jnp.where(upper, pieces[1], pieces[2]), 0.0)
        sent[s, 16:24] = jnp.where(keep, pieces[3], 0.0)

    second = []
    for k in range(1, 16):
        s = lax.rem(g + k, 16)
        copy = pltpu.make_async_remote_copy(
            src_ref=sent.at[s],
            dst_ref=video.at[g],
            send_sem=send2.at[k],
            recv_sem=recv2.at[k],
            device_id=(o, s),
            device_id_type=MESH,
        )
        copy.start()
        second.append(copy)
    own = pltpu.make_async_copy(sent.at[g], video.at[g], own_sem)
    own.start()
    own.wait()
    for copy in second:
        copy.wait()


def encode_kernel(
    position, video, u, we, wb, cols, off,
    out, x3, entry, xs, sums, mixed, zs, turned,
):
    o, s = position()
    lane = iota((1, LANES), 1)
    c4, t = lane // 64, lane % 16
    col = COLS * s + 4 * (t - 1) + c4
    in_frame = jnp.where((col >= 0) & (col < W), 1.0, 0.0)
    low = iota((16, 128), 1) < 64

    low8 = iota((24, 128), 1) < 64
    lines = []
    for f in range(FRAMES):
        wide = jnp.concatenate(
            [
                jnp.where(low8, video[f], video[4 + f]),
                jnp.where(low8, video[8 + f], video[12 + f]),
            ],
            axis=1,
        )
        hi = wide.astype(BF16).astype(F32)
        lines += [hi, wide - hi]
    k = iota((LANES, LANES), 0)
    j = iota((LANES, LANES), 1)
    source = j % 64 // 16 * 64 + 4 * (j % 16) + j // 64
    permute = jnp.where(k == source, 1.0, 0.0).astype(BF16)
    placed = dot(jnp.concatenate(lines, axis=0).astype(BF16), permute)

    def shifted(v0, v1, select):
        b10, b32 = pltpu.roll(v0, 64, 1), pltpu.roll(v1, 64, 1)
        b3s, b0s = pltpu.roll(v1, 65, 1), pltpu.roll(v0, 63, 1)
        left = jnp.where(select, b3s, b10)
        middle = jnp.where(select, b10, b32)
        right = jnp.where(select, b32, b0s)
        return left, middle, right

    for f in range(FRAMES):
        block = placed[48 * f : 48 * f + 48]
        v0, v1 = block[:, 0:128], block[:, 128:256]
        left, middle, right = shifted(v0, v1, iota((48, 128), 1) < 64)
        taps = []
        for a, b in ((left, middle), (v0, v1), (middle, right)):
            both = jnp.concatenate([a, b], axis=1)
            taps += [both, both[0:24]]
        taps.append(jnp.zeros((40, LANES), F32))
        x3[pl.ds(f * LANES, LANES), :] = jnp.concatenate(taps, axis=0).astype(BF16)

    def entry_of(f):
        first = max(0, f - 2)
        k0 = (2 - (f - first)) * LANES
        entry[f] = dot(we[:, k0:], x3[pl.ds(first * LANES, (f - first + 1) * LANES), :])
        inverse = []
        for re in range(6):
            total = jnp.zeros((8, LANES), F32)
            for c in range(0, CH, 8):
                value = entry[f, pl.ds(re * CH + c, 8), :] + off[pl.ds(c, 8), :]
                entry[f, pl.ds(re * CH + c, 8), :] = value
                total = total + value * value
            mean = jnp.sum(total, axis=0, keepdims=True) * (1 / CH)
            scale = lax.rsqrt(mean + EPSILON) * in_frame
            if re == 0:
                scale = scale * jnp.where(o > 0, 1.0, 0.0)
            if re == 5:
                scale = scale * jnp.where(o < N_DP - 1, 1.0, 0.0)
            inverse.append(scale)

        def group(i, _):
            at = pl.multiple_of(i * 16, 16)
            gain = cols[pl.ds(at, 16), 5:6] * 0.5
            act = []
            for re in range(6):
                v = entry[f, pl.ds(re * CH + at, 16), :] * inverse[re] * gain
                act.append(v + v * jnp.tanh(v))
            d0, d1, d2, d3, d4, d5 = act
            a, b = d4 - 4 * d2, d3 - 4 * d1
            c, e = d4 - d2, 2 * (d3 - d1)
            made = (4 * d0 - 5 * d2 + d4, a + b, a - b, c + e, c - e, 4 * d1 - 5 * d3 + d5)
            for w in range(6):
                v0, v1 = made[w][:, 0:128], made[w][:, 128:256]
                left, middle, right = shifted(v0, v1, low)
                his, los = zip(*[halves(x) for x in (left, middle, right, v0, v1)])
                for d, (p, q) in enumerate(((0, 1), (3, 4), (1, 2))):
                    for part, source in enumerate((his, los, his)):
                        rows = pl.ds((part * 3 + d) * CH + at, 16)
                        xs[w, rows, 0:128] = source[p]
                        xs[w, rows, 128:256] = source[q]
            return 0

        lax.fori_loop(0, CH // 16, group, 0)

    def middle_of(f):
        reach = min(3, FRAMES - f)

        def step(w, _):
            y = dot(u[w, 0 : reach * CH, :], xs[w])
            for later in range(reach):
                part = y[later * CH : (later + 1) * CH]
                if f == 0 or later == 2:
                    sums[f + later, w] = part
                else:
                    sums[f + later, w] = sums[f + later, w] + part
            return 0

        lax.fori_loop(0, 6, step, 0)

    def latent_of(f):
        def group(i, totals):
            at = pl.multiple_of(i * 16, 16)
            bias = cols[pl.ds(at, 16), 6:7]
            y = [sums[f, w, pl.ds(at, 16), :] for w in range(6)]
            s12, d12, s34, d34 = y[1] + y[2], y[1] - y[2], y[3] + y[4], y[3] - y[4]
            made = (y[0] + s12 + s34, d12 + 2 * d34, s12 + 4 * s34, d12 + 8 * d34 + y[5])
            fresh = []
            for r in range(4):
                v = entry[f, pl.ds((r + 1) * CH + at, 16), :] + bias + made[r]
                mixed[r, pl.ds(at, 16), :] = v
                fresh.append(totals[r] + v * v)
            return tuple(fresh)

        zero = jnp.zeros((16, LANES), F32)
        totals = lax.fori_loop(0, CH // 16, group, (zero,) * 4)
        inverse = [
            lax.rsqrt(jnp.sum(x, axis=0, keepdims=True) * (1 / CH) + EPSILON) for x in totals
        ]
        side = pl.ds(f % 2 * 128, 128)

        def finish(i, _):
            at = pl.multiple_of(i * 16, 16)
            gain = cols[pl.ds(at, 16), 7:8] * 0.5
            act = []
            for r in range(4):
                v = mixed[r, pl.ds(at, 16), :] * inverse[r] * gain
                act.append(v + v * jnp.tanh(v))
            for r in range(2):
                for pair in range(2):
                    p0 = act[r][:, pair * 128 : pair * 128 + 128]
                    p1 = act[2 + r][:, pair * 128 : pair * 128 + 128]
                    even = jnp.where(low, p0, pltpu.roll(p1, 64, 1))
                    odd = jnp.where(low, pltpu.roll(p0, 64, 1), p1)
                    for c, x in ((2 * pair, even), (2 * pair + 1, odd)):
                        hi, lo = halves(x)
                        rows = pl.ds((c * 2 + r) * CH + at, 16)
                        zs[0, rows, side] = hi
                        zs[1, rows, side] = lo
            return 0

        lax.fori_loop(0, CH // 16, finish, 0)

    def tokens_of(f):
        both = dot(wb[...], zs[0])
        bias = jnp.concatenate([cols[:, 8:9], cols[0:32, 9:10]], axis=0)
        made = both[0:128] + both[128:256] + dot(wb[0:128], zs[1]) + bias
        turned[...] = jnp.transpose(made)
        for side in range(2):
            for clip in range(CLIPS):
                for t in range(13):
                    rows = pl.ds(side * 128 + clip * 16 + t + 1, 2, stride=64)
                    out[clip * 4 + f - 1 + side, :, pl.ds(t * 128, 128)] = turned[rows, :]

    for f in range(FRAMES):
        entry_of(f)
        middle_of(f)
        latent_of(f)
        if f % 2:
            tokens_of(f)


def shape(dims, dtype):
    return jax.ShapeDtypeStruct(dims, dtype)


MADE = (
    shape((6, 3 * CH, MID_K), BF16),
    shape((6 * CH, 3 * LANES), BF16),
    shape((256, 8 * CH), BF16),
    shape((CH, 128), F32),
    shape((CH, LANES), F32),
)
VMEM = pl.BlockSpec(memory_space=pltpu.VMEM)
SMEM = pl.BlockSpec(memory_space=pltpu.SMEM)
ENCODE_SCRATCH = [
    pltpu.VMEM((FRAMES * LANES, LANES), BF16),
    pltpu.VMEM((FRAMES, 6 * CH, LANES), F32),
    pltpu.VMEM((6, MID_K, LANES), BF16),
    pltpu.VMEM((FRAMES, 6, CH, LANES), F32),
    pltpu.VMEM((4, CH, LANES), F32),
    pltpu.VMEM((2, 8 * CH, LANES), BF16),
    pltpu.VMEM((LANES, 128), F32),
]


def where_am_i():
    return lax.axis_index("dp"), lax.axis_index("seq")


def body(
    loaded, tile_rows, bucket_ids, in_weight, in_bias, bucket_bias, norm_gain, mid_weight,
    mid_bias, head_gain, head_weight, head_bias,
):
    def line(x):
        return x.reshape(1, -1)

    video, *made = pl.pallas_call(
        exchange_kernel,
        out_shape=(shape((NF, 24, 128), F32),) + MADE,
        in_specs=[VMEM, SMEM, SMEM] + [VMEM] * 9,
        out_specs=(pl.BlockSpec(memory_space=pl.ANY),) + (VMEM,) * 5,
        scratch_shapes=[
            pltpu.VMEM((128, TILE), F32),
            pltpu.VMEM((24, TILE + 256), F32),
            pltpu.VMEM((N_SEQ, 24, 128), F32),
            pltpu.SemaphoreType.DMA((16,)),
            pltpu.SemaphoreType.DMA((16,)),
            pltpu.SemaphoreType.DMA((16,)),
            pltpu.SemaphoreType.DMA((16,)),
            pltpu.SemaphoreType.DMA,
        ],
        compiler_params=pltpu.CompilerParams(
            collective_id=0, has_side_effects=True, vmem_limit_bytes=40 * 2**20
        ),
    )(
        loaded, tile_rows, bucket_ids, in_weight, line(in_bias), bucket_bias, line(norm_gain),
        mid_weight, line(mid_bias), line(head_gain), head_weight, line(head_bias),
    )
    return pl.pallas_call(
        functools.partial(encode_kernel, where_am_i),
        out_shape=shape((NF, 2, TILE), F32),
        in_specs=[VMEM] * 6,
        out_specs=VMEM,
        scratch_shapes=ENCODE_SCRATCH,
        compiler_params=pltpu.CompilerParams(vmem_limit_bytes=48 * 2**20),
    )(video, *made)


def solution(mesh):
    return jax.shard_map(
        body,
        mesh=mesh,
        in_specs=(P("seq", "dp", None), P("seq", "dp")) + (P(),) * 10,
        out_specs=P(None, "dp", "seq"),
        check_vma=False,
    )
```

```python
import functools

import jax
import jax.numpy as jnp
from jax import lax
from jax.experimental import pallas as pl
from jax.experimental.pallas import tpu as pltpu
from jax.sharding import PartitionSpec as P

F32, BF16, I32 = jnp.float32, jnp.bfloat16, jnp.int32
MESH = pl.DeviceIdType.MESH
EPSILON = 1e-06
CH = 96
ZCH = 16
W = 832
NF = 16
FRAMES = 4
CLIPS = 4
N_DP = 16
N_SEQ = 16
COLS = W // N_SEQ
TILE = 2 * W
LANES = 256
MID_K = 9 * CH

G43 = (
    (1 / 4, 0.0, 0.0),
    (-1 / 6, -1 / 6, -1 / 6),
    (-1 / 6, 1 / 6, -1 / 6),
    (1 / 24, 1 / 12, 1 / 6),
    (1 / 24, -1 / 12, 1 / 6),
    (0.0, 0.0, 1.0),
)


def iota(shape, dim):
    return lax.broadcasted_iota(I32, shape, dim)


def dot(a, b):
    return jnp.dot(a, b, preferred_element_type=F32)


def halves(x):
    hi = x.astype(BF16)
    return hi, (x - hi.astype(F32)).astype(BF16)


def prepare(
    ids, in_weight, in_bias, bucket_bias, norm_gain, mid_weight, mid_bias, head_gain,
    head_weight, head_bias, u, we, wb, cols, off, end,
):
    for a in range(3):
        for d in range(3):
            taps = [mid_weight[9 * a + 3 * b + d] for b in range(3)]
            outer, inner = taps[0] + taps[2], taps[1]
            s4 = taps[0] * (1 / 24) + taps[2] * (1 / 6)
            made = (
                taps[0] * 0.25,
                (outer + inner) * (-1 / 6),
                (inner - outer) * (1 / 6),
                s4 + inner * (1 / 12),
                s4 - inner * (1 / 12),
                taps[2],
            )
            for w in range(6):
                hi, lo = halves(made[w])
                rows = pl.ds((2 - a) * CH, CH)
                u[w, rows, pl.ds(d * CH, CH)] = hi
                u[w, rows, pl.ds((3 + d) * CH, CH)] = hi
                u[w, rows, pl.ds((6 + d) * CH, CH)] = lo
    n = iota((81, LANES), 1)
    d, part, h, m = n // 72, n % 72 // 24, n % 24 // 12, n % 12
    key = 3 * d + m % 3
    row = 2 * (m // 3) + h
    first = n < 216
    k = iota((81, LANES), 0)
    whi, wlo = halves(jnp.transpose(in_weight[...]))
    for re in range(6):
        b = row - re
        legal = first & (b >= 0) & (b <= 2)
        for a in range(3):
            hit = legal & (k == 27 * a + 9 * b + key)
            e01 = jnp.where(hit & (part < 2), 1.0, 0.0).astype(BF16)
            e2 = jnp.where(hit & (part == 2), 1.0, 0.0).astype(BF16)
            got = dot(whi, e01) + dot(wlo, e2)
            we[pl.ds(re * CH, CH), pl.ds(a * LANES, LANES)] = got.astype(BF16)
    lines = jnp.concatenate(
        [in_bias[...], bucket_bias[...], norm_gain[...], mid_bias[...], head_gain[...]], axis=0
    )
    table = jnp.transpose(lines)
    for i, (at, scale) in enumerate(((5, 0.5), (6, 1.0), (7, 0.5))):
        cols[i] = jnp.broadcast_to(table[:, at : at + 1] * scale, (CH, 128))
    clip = iota((CH, LANES), 1) % 64 // 16
    total = jnp.broadcast_to(table[:, 0:1], (CH, LANES))
    for c in range(CLIPS):
        mine = sum(
            table[:, 1 + b : 2 + b] * jnp.where(ids[c] == b, 1.0, 0.0) for b in range(4)
        )
        total = total + jnp.where(clip == c, mine, 0.0)
    off[...] = total
    line = iota((128, ZCH), 0)
    spread = jnp.where(line % 64 // 4 == iota((128, ZCH), 1), 1.0, 0.0)
    hhi, hlo = halves(head_weight[...])
    line = iota((128, CH), 0)
    for part, piece in enumerate((hhi, hlo)):
        wide = dot(spread.astype(BF16), piece)
        for c4 in range(4):
            for r in range(2):
                q2, s = c4 // 2, c4 % 2
                keep = (line // 64 == q2) & (line % 2 == s) & (line % 4 // 2 == r)
                at = (c4 * 2 + r) * CH
                wb[pl.ds(part * 128, 128), pl.ds(at, CH)] = jnp.where(keep, wide, 0.0).astype(BF16)
    hb = jnp.sum(spread * head_bias[...], axis=1, keepdims=True)
    end[...] = jnp.broadcast_to(hb, (128, 128))


def exchange_kernel(
    loaded, tile_rows, bucket_ids, in_weight, in_bias, bucket_bias, norm_gain, mid_weight, mid_bias,
    head_gain, head_weight, head_bias,
    video, u, we, wb, cols, off, end,
    raw, numbers_smem, ids, weight_in, bias_in, buckets, gain1, weight_mid, bias_mid, gain2,
    weight_head, bias_head, in_sems,
    got, picked, sent, send1, recv1, send2, recv2, own_sem,
):
    o, g = lax.axis_index("dp"), lax.axis_index("seq")
    sources = (
        loaded, tile_rows, bucket_ids, in_weight, in_bias, bucket_bias, norm_gain, mid_weight,
        mid_bias, head_gain, head_weight, head_bias,
    )
    targets = (
        raw, numbers_smem, ids, weight_in, bias_in, buckets, gain1, weight_mid, bias_mid, gain2,
        weight_head, bias_head,
    )
    loads = [
        pltpu.make_async_copy(a, b, in_sems.at[i]) for i, (a, b) in enumerate(zip(sources, targets))
    ]
    for load in loads:
        load.start()
    barrier = pltpu.get_barrier_semaphore()
    for k in range(1, 16):
        pl.semaphore_signal(barrier, 1, device_id=(lax.rem(o + k, 16), g), device_id_type=MESH)
        pl.semaphore_signal(barrier, 1, device_id=(o, lax.rem(g + k, 16)), device_id_type=MESH)

    loads[0].wait()
    loads[1].wait()
    here = pl.ds(pl.multiple_of(o * 8, 8), 8)
    lane = iota((1, TILE), 1)
    numbers = jnp.full((1, TILE), -1000.0, F32)
    for j in range(6):
        numbers = jnp.where(lane == 8 * o + j, numbers_smem[0, j].astype(F32), numbers)
    got[here, :] = jnp.concatenate(
        [raw[j] for j in range(6)] + [numbers, jnp.zeros((1, TILE), F32)], axis=0
    )
    pl.semaphore_wait(barrier, 30)

    first = []
    for k in range(1, 16):
        copy = pltpu.make_async_remote_copy(
            src_ref=got.at[here],
            dst_ref=got.at[here],
            send_sem=send1.at[k],
            recv_sem=recv1.at[k],
            device_id=(lax.rem(o + k, 16), g),
            device_id_type=MESH,
        )
        copy.start()
        first.append(copy)

    for load in loads[2:]:
        load.wait()
    prepare(
        ids, weight_in, bias_in, buckets, gain1, weight_mid, bias_mid, gain2, weight_head,
        bias_head, u, we, wb, cols, off, end,
    )

    for copy in first:
        copy.wait()

    label = got[pl.ds(6, 1), 0:128]
    for l in range(1, 16):
        label = jnp.maximum(label, got[pl.ds(8 * l + 6, 1), 0:128])
    m = iota((24, 128), 0) % 12
    pg, c = m // 3, m % 3
    wanted = 6 * o + 6 * ((pg + 1) // 2 - 1) + 2 * c + (pg + 1) % 2
    hot = jnp.where(label == wanted.astype(F32), 1.0, 0.0).astype(BF16)
    hot2 = jnp.concatenate([hot, hot], axis=1)
    picked[:, 0:128] = jnp.zeros((24, 128), F32)
    picked[:, 128 + TILE :] = jnp.zeros((24, 128), F32)
    for at in range(0, TILE, 128):
        hi, lo = halves(got[:, at : at + 128])
        picked[:, 128 + at : 256 + at] = dot(hot2, jnp.concatenate([hi, lo], axis=0))

    half = lax.rem(g // FRAMES, 2) * 64
    lane = iota((8, 128), 1) - half
    inside = (lane >= 0) & (lane < 64)
    upper = iota((8, 128), 0) < 4
    for s in range(N_SEQ):
        col = lane + (COLS * s - 4)
        keep = inside & (col >= 0) & (col < W)
        pieces = []
        for h, rows in ((0, 0), (0, 8), (1, 8), (1, 16)):
            start = 128 + h * W + COLS * s - 4
            base = start // 128 * 128
            wide = picked[rows : rows + 8, base : base + 256]
            turned = pltpu.roll(wide, lax.rem(half + 256 - (start - base), 256), 1)
            pieces.append(turned[:, 0:128])
        sent[s, 0:8] = jnp.where(keep, pieces[0], 0.0)
        sent[s, 8:16] = jnp.where(keep, jnp.where(upper, pieces[1], pieces[2]), 0.0)
        sent[s, 16:24] = jnp.where(keep, pieces[3], 0.0)

    second = []
    for k in range(1, 16):
        s = lax.rem(g + k, 16)
        copy = pltpu.make_async_remote_copy(
            src_ref=sent.at[s],
            dst_ref=video.at[g],
            send_sem=send2.at[k],
            recv_sem=recv2.at[k],
            device_id=(o, s),
            device_id_type=MESH,
        )
        copy.start()
        second.append(copy)
    own = pltpu.make_async_copy(sent.at[g], video.at[g], own_sem)
    own.start()
    own.wait()
    for copy in second:
        copy.wait()


def encode_kernel(
    position, video, u, we, wb, cols, off, end,
    out, x3, entry, xs, sums, mixed, zs, turned,
):
    o, s = position()
    lane = iota((1, LANES), 1)
    c4, t = lane // 64, lane % 16
    col = COLS * s + 4 * (t - 1) + c4
    in_frame = jnp.where((col >= 0) & (col < W), 1.0, 0.0)
    low = iota((16, 128), 1) < 64

    low8 = iota((24, 128), 1) < 64
    lines = []
    for f in range(FRAMES):
        wide = jnp.concatenate(
            [
                jnp.where(low8, video[f], video[4 + f]),
                jnp.where(low8, video[8 + f], video[12 + f]),
            ],
            axis=1,
        )
        hi = wide.astype(BF16).astype(F32)
        lines += [hi, wide - hi]
    k = iota((LANES, LANES), 0)
    j = iota((LANES, LANES), 1)
    source = j % 64 // 16 * 64 + 4 * (j % 16) + j // 64
    permute = jnp.where(k == source, 1.0, 0.0).astype(BF16)
    placed = dot(jnp.concatenate(lines, axis=0).astype(BF16), permute)

    def wide_column(which, at):
        column = cols[which, pl.ds(at, 16), :]
        return jnp.concatenate([column, column], axis=1)

    def shifted(v0, v1, select):
        b10, b32 = pltpu.roll(v0, 64, 1), pltpu.roll(v1, 64, 1)
        b3s, b0s = pltpu.roll(v1, 65, 1), pltpu.roll(v0, 63, 1)
        left = jnp.where(select, b3s, b10)
        middle = jnp.where(select, b10, b32)
        right = jnp.where(select, b32, b0s)
        return left, middle, right

    for f in range(FRAMES):
        block = placed[48 * f : 48 * f + 48]
        v0, v1 = block[:, 0:128], block[:, 128:256]
        left, middle, right = shifted(v0, v1, iota((48, 128), 1) < 64)
        taps = []
        for a, b in ((left, middle), (v0, v1), (middle, right)):
            both = jnp.concatenate([a, b], axis=1)
            taps += [both, both[0:24]]
        taps.append(jnp.zeros((40, LANES), F32))
        x3[pl.ds(f * LANES, LANES), :] = jnp.concatenate(taps, axis=0).astype(BF16)

    def entry_of(f):
        first = max(0, f - 2)
        k0 = (2 - (f - first)) * LANES
        entry[f] = dot(we[:, k0:], x3[pl.ds(first * LANES, (f - first + 1) * LANES), :])
        inverse = []
        for re in range(6):
            total = jnp.zeros((8, LANES), F32)
            for c in range(0, CH, 8):
                value = entry[f, pl.ds(re * CH + c, 8), :] + off[pl.ds(c, 8), :]
                entry[f, pl.ds(re * CH + c, 8), :] = value
                total = total + value * value
            mean = jnp.sum(total, axis=0, keepdims=True) * (1 / CH)
            scale = lax.rsqrt(mean + EPSILON) * in_frame
            if re == 0:
                scale = scale * jnp.where(o > 0, 1.0, 0.0)
            if re == 5:
                scale = scale * jnp.where(o < N_DP - 1, 1.0, 0.0)
            inverse.append(scale)

        def group(i, _):
            at = i * 16
            gain = wide_column(0, at)
            act = []
            for re in range(6):
                v = entry[f, pl.ds(re * CH + at, 16), :] * inverse[re] * gain
                act.append(v + v * jnp.tanh(v))
            d0, d1, d2, d3, d4, d5 = act
            a, b = d4 - 4 * d2, d3 - 4 * d1
            c, e = d4 - d2, 2 * (d3 - d1)
            made = (4 * d0 - 5 * d2 + d4, a + b, a - b, c + e, c - e, 4 * d1 - 5 * d3 + d5)
            for w in range(6):
                v0, v1 = made[w][:, 0:128], made[w][:, 128:256]
                left, middle, right = shifted(v0, v1, low)
                his, los = zip(*[halves(x) for x in (left, middle, right, v0, v1)])
                for d, (p, q) in enumerate(((0, 1), (3, 4), (1, 2))):
                    for part, source in enumerate((his, los, his)):
                        rows = pl.ds((part * 3 + d) * CH + at, 16)
                        xs[f, w, rows, 0:128] = source[p]
                        xs[f, w, rows, 128:256] = source[q]
            return 0

        lax.fori_loop(0, CH // 16, group, 0, unroll=True)

    def middle_of(f):
        reach = min(3, FRAMES - f)

        def step(w, _):
            y = dot(u[w, 0 : reach * CH, :], xs[f, w])
            for later in range(reach):
                part = y[later * CH : (later + 1) * CH]
                if f == 0 or later == 2:
                    sums[f + later, w] = part
                else:
                    sums[f + later, w] = sums[f + later, w] + part
            return 0

        lax.fori_loop(0, 6, step, 0, unroll=True)

    def latent_of(f):
        def group(i, totals):
            at = i * 16
            bias = wide_column(1, at)
            y = [sums[f, w, pl.ds(at, 16), :] for w in range(6)]
            s12, d12, s34, d34 = y[1] + y[2], y[1] - y[2], y[3] + y[4], y[3] - y[4]
            made = (y[0] + s12 + s34, d12 + 2 * d34, s12 + 4 * s34, d12 + 8 * d34 + y[5])
            fresh = []
            for r in range(4):
                v = entry[f, pl.ds((r + 1) * CH + at, 16), :] + bias + made[r]
                mixed[f, r, pl.ds(at, 16), :] = v
                fresh.append(totals[r] + v * v)
            return tuple(fresh)

        zero = jnp.zeros((16, LANES), F32)
        totals = lax.fori_loop(0, CH // 16, group, (zero,) * 4, unroll=True)
        inverse = [
            lax.rsqrt(jnp.sum(x, axis=0, keepdims=True) * (1 / CH) + EPSILON) for x in totals
        ]
        side = pl.ds(f % 2 * 128, 128)

        def finish(i, _):
            at = i * 16
            gain = wide_column(2, at)
            act = []
            for r in range(4):
                v = mixed[f, r, pl.ds(at, 16), :] * inverse[r] * gain
                act.append(v + v * jnp.tanh(v))
            for r in range(2):
                for pair in range(2):
                    p0 = act[r][:, pair * 128 : pair * 128 + 128]
                    p1 = act[2 + r][:, pair * 128 : pair * 128 + 128]
                    even = jnp.where(low, p0, pltpu.roll(p1, 64, 1))
                    odd = jnp.where(low, pltpu.roll(p0, 64, 1), p1)
                    for c, x in ((2 * pair, even), (2 * pair + 1, odd)):
                        hi, lo = halves(x)
                        rows = pl.ds((c * 2 + r) * CH + at, 16)
                        zs[f // 2, 0, rows, side] = hi
                        zs[f // 2, 1, rows, side] = lo
            return 0

        lax.fori_loop(0, CH // 16, finish, 0, unroll=True)

    def tokens_of(f):
        both = dot(wb[...], zs[f // 2, 0])
        bias = jnp.concatenate([end[...], end[...]], axis=1)
        made = both[0:128] + both[128:256] + dot(wb[0:128], zs[f // 2, 1]) + bias
        turned[f // 2] = jnp.transpose(made)
        for side in range(2):
            for clip in range(CLIPS):
                for t in range(13):
                    rows = pl.ds(side * 128 + clip * 16 + t + 1, 2, stride=64)
                    out[clip * 4 + f - 1 + side, :, pl.ds(t * 128, 128)] = turned[f // 2, rows, :]

    entry_of(0)
    for f in range(FRAMES):
        if f + 1 < FRAMES:
            entry_of(f + 1)
        middle_of(f)
        latent_of(f)
        if f % 2:
            tokens_of(f)


def shape(dims, dtype):
    return jax.ShapeDtypeStruct(dims, dtype)


MADE = (
    shape((6, 3 * CH, MID_K), BF16),
    shape((6 * CH, 3 * LANES), BF16),
    shape((256, 8 * CH), BF16),
    shape((3, CH, 128), F32),
    shape((CH, LANES), F32),
    shape((128, 128), F32),
)
VMEM_BYTES = 60 * 2**20
VMEM = pl.BlockSpec(memory_space=pltpu.VMEM)
HBM = pl.BlockSpec(memory_space=pltpu.HBM)
ENCODE_SCRATCH = [
    pltpu.VMEM((FRAMES * LANES, LANES), BF16),
    pltpu.VMEM((FRAMES, 6 * CH, LANES), F32),
    pltpu.VMEM((FRAMES, 6, MID_K, LANES), BF16),
    pltpu.VMEM((FRAMES, 6, CH, LANES), F32),
    pltpu.VMEM((FRAMES, 4, CH, LANES), F32),
    pltpu.VMEM((2, 2, 8 * CH, LANES), BF16),
    pltpu.VMEM((2, LANES, 128), F32),
]


def whole_kernel(*refs):
    args, out, (made, exchange, encode) = refs[:12], refs[12], refs[13:]
    exchange_kernel(*args, *made, *exchange)
    encode_kernel(where_am_i, *made, out, *encode)


def where_am_i():
    return lax.axis_index("dp"), lax.axis_index("seq")


def body(
    loaded, tile_rows, bucket_ids, in_weight, in_bias, bucket_bias, norm_gain, mid_weight,
    mid_bias, head_gain, head_weight, head_bias,
):
    def line(x):
        return x.reshape(1, -1)

    return pl.pallas_call(
        whole_kernel,
        out_shape=shape((NF, 2, TILE), F32),
        in_specs=[HBM] * 12,
        out_specs=VMEM,
        scratch_shapes=[
            [pltpu.VMEM((NF, 24, 128), F32)] + [pltpu.VMEM(x.shape, x.dtype) for x in MADE],
            [
                pltpu.VMEM((6, 1, TILE), F32),
                pltpu.SMEM((1, 6), I32),
                pltpu.SMEM((4,), I32),
                pltpu.VMEM((81, CH), F32),
                pltpu.VMEM((1, CH), F32),
                pltpu.VMEM((4, CH), F32),
                pltpu.VMEM((1, CH), F32),
                pltpu.VMEM((27, CH, CH), F32),
                pltpu.VMEM((1, CH), F32),
                pltpu.VMEM((1, CH), F32),
                pltpu.VMEM((ZCH, CH), F32),
                pltpu.VMEM((1, ZCH), F32),
                pltpu.SemaphoreType.DMA((12,)),
                pltpu.VMEM((128, TILE), F32),
                pltpu.VMEM((24, TILE + 256), F32),
                pltpu.VMEM((N_SEQ, 24, 128), F32),
                pltpu.SemaphoreType.DMA((16,)),
                pltpu.SemaphoreType.DMA((16,)),
                pltpu.SemaphoreType.DMA((16,)),
                pltpu.SemaphoreType.DMA((16,)),
                pltpu.SemaphoreType.DMA,
            ],
            ENCODE_SCRATCH,
        ],
        compiler_params=pltpu.CompilerParams(
            collective_id=0, has_side_effects=True, vmem_limit_bytes=VMEM_BYTES
        ),
    )(
        jnp.transpose(loaded, (1, 0, 2)), tile_rows, bucket_ids, in_weight.T, line(in_bias), bucket_bias, line(norm_gain),
        mid_weight, line(mid_bias), line(head_gain), head_weight, line(head_bias),
    )


def solution(mesh):
    return jax.shard_map(
        body,
        mesh=mesh,
        in_specs=(P("seq", "dp", None), P("seq", "dp")) + (P(),) * 10,
        out_specs=P(None, "dp", "seq"),
        check_vma=False,
    )
```

```python
import functools

import jax
import jax.numpy as jnp
from jax import lax
from jax.experimental import pallas as pl
from jax.experimental.pallas import tpu as pltpu
from jax.sharding import PartitionSpec as P

F32, BF16, I32 = jnp.float32, jnp.bfloat16, jnp.int32
MESH = pl.DeviceIdType.MESH
EPSILON = 1e-06
CH = 96
ZCH = 16
W = 832
NF = 16
FRAMES = 4
CLIPS = 4
N_DP = 16
N_SEQ = 16
COLS = W // N_SEQ
TILE = 2 * W
LANES = 256
MID_K = 9 * CH
PIECES = (0, 6, 7, 1, 8, 2, 9, 3, 10, 4, 11, 5, 12)
CHUNKS = ((0, 31), (31, 24), (55, 24))
WINDOWS = (4, 5, 7)


G43 = (
    (1 / 4, 0.0, 0.0),
    (-1 / 6, -1 / 6, -1 / 6),
    (-1 / 6, 1 / 6, -1 / 6),
    (1 / 24, 1 / 12, 1 / 6),
    (1 / 24, -1 / 12, 1 / 6),
    (0.0, 0.0, 1.0),
)


def iota(shape, dim):
    return lax.broadcasted_iota(I32, shape, dim)


def dot(a, b):
    return jnp.dot(a, b, preferred_element_type=F32)


def halves(x):
    hi = x.astype(BF16)
    return hi, (x - hi.astype(F32)).astype(BF16)


def prepare(
    ids, in_weight, in_bias, bucket_bias, norm_gain, mid_weight, mid_bias, head_gain,
    head_weight, head_bias, u, we, wb, cols, off, end,
):
    for a in range(3):
        for d in range(3):
            taps = [mid_weight[9 * a + 3 * b + d] for b in range(3)]
            outer, inner = taps[0] + taps[2], taps[1]
            s4 = taps[0] * (1 / 24) + taps[2] * (1 / 6)
            made = (
                taps[0] * 0.25,
                (outer + inner) * (-1 / 6),
                (inner - outer) * (1 / 6),
                s4 + inner * (1 / 12),
                s4 - inner * (1 / 12),
                taps[2],
            )
            for w in range(6):
                hi, lo = halves(made[w])
                rows = pl.ds((2 - a) * CH, CH)
                u[w, rows, pl.ds(d * CH, CH)] = hi
                u[w, rows, pl.ds((3 + d) * CH, CH)] = hi
                u[w, rows, pl.ds((6 + d) * CH, CH)] = lo
    n = iota((81, LANES), 1)
    d, part, h, m = n // 72, n % 72 // 24, n % 24 // 12, n % 12
    key = 3 * d + m % 3
    row = 2 * (m // 3) + h
    first = n < 216
    k = iota((81, LANES), 0)
    whi, wlo = halves(jnp.transpose(in_weight[...]))
    for re in range(6):
        b = row - re
        legal = first & (b >= 0) & (b <= 2)
        for a in range(3):
            hit = legal & (k == 27 * a + 9 * b + key)
            e01 = jnp.where(hit & (part < 2), 1.0, 0.0).astype(BF16)
            e2 = jnp.where(hit & (part == 2), 1.0, 0.0).astype(BF16)
            got = dot(whi, e01) + dot(wlo, e2)
            we[pl.ds(re * CH, CH), pl.ds(a * LANES, LANES)] = got.astype(BF16)
    lines = jnp.concatenate(
        [in_bias[...], bucket_bias[...], norm_gain[...], mid_bias[...], head_gain[...]], axis=0
    )
    table = jnp.transpose(lines)
    for i, (at, scale) in enumerate(((5, 0.5), (6, 1.0), (7, 0.5))):
        cols[i] = jnp.broadcast_to(table[:, at : at + 1] * scale, (CH, 128))
    clip = iota((CH, LANES), 1) % 64 // 16
    total = jnp.broadcast_to(table[:, 0:1], (CH, LANES))
    for c in range(CLIPS):
        mine = sum(
            table[:, 1 + b : 2 + b] * jnp.where(ids[c] == b, 1.0, 0.0) for b in range(4)
        )
        total = total + jnp.where(clip == c, mine, 0.0)
    off[...] = total
    line = iota((128, ZCH), 0)
    spread = jnp.where(line % 64 // 4 == iota((128, ZCH), 1), 1.0, 0.0)
    hhi, hlo = halves(head_weight[...])
    line = iota((128, CH), 0)
    for part, piece in enumerate((hhi, hlo)):
        wide = dot(spread.astype(BF16), piece)
        for c4 in range(4):
            for r in range(2):
                q2, s = c4 // 2, c4 % 2
                keep = (line // 64 == q2) & (line % 2 == s) & (line % 4 // 2 == r)
                at = (c4 * 2 + r) * CH
                wb[pl.ds(part * 128, 128), pl.ds(at, CH)] = jnp.where(keep, wide, 0.0).astype(BF16)
    hb = jnp.sum(spread * head_bias[...], axis=1, keepdims=True)
    end[...] = jnp.broadcast_to(hb, (128, 128))


def exchange_kernel(
    loaded, tile_rows, bucket_ids, in_weight, in_bias, bucket_bias, norm_gain, mid_weight, mid_bias,
    head_gain, head_weight, head_bias,
    video, u, we, wb, cols, off, end,
    raw, numbers_smem, ids, weight_in, bias_in, buckets, gain1, weight_mid, bias_mid, gain2,
    weight_head, bias_head, in_sems,
    got, picked, sent, send1, recv1, send2, recv2, own_sem,
):
    o, g = lax.axis_index("dp"), lax.axis_index("seq")
    sources = (
        loaded, tile_rows, bucket_ids, in_weight, in_bias, bucket_bias, norm_gain, mid_weight,
        mid_bias, head_gain, head_weight, head_bias,
    )
    targets = (
        raw, numbers_smem, ids, weight_in, bias_in, buckets, gain1, weight_mid, bias_mid, gain2,
        weight_head, bias_head,
    )
    loads = [
        pltpu.make_async_copy(a, b, in_sems.at[i]) for i, (a, b) in enumerate(zip(sources, targets))
    ]
    for load in loads:
        load.start()
    barrier = pltpu.get_barrier_semaphore()
    for k in range(1, 16):
        pl.semaphore_signal(barrier, 1, device_id=(lax.rem(o + k, 16), g), device_id_type=MESH)
        pl.semaphore_signal(barrier, 1, device_id=(o, lax.rem(g + k, 16)), device_id_type=MESH)

    loads[0].wait()
    loads[1].wait()
    lane = iota((1, 128), 1)
    numbers = jnp.full((1, 128), -1000.0, F32)
    for j in range(6):
        numbers = jnp.where(lane == 8 * o + j, numbers_smem[0, j].astype(F32), numbers)
        for at, t in enumerate(PIECES):
            got[o, pl.ds(1 + 6 * at + j, 1), :] = raw[j, :, t * 128 : t * 128 + 128]
    got[o, 0:1, :] = numbers
    picked[:, 0:128] = jnp.zeros((16, 128), F32)
    picked[:, 128 + TILE :] = jnp.zeros((16, 128), F32)
    pl.semaphore_wait(barrier, 30)

    for c, (start, rows) in enumerate(CHUNKS):
        part = got.at[o, pl.ds(start, rows)]
        for k in range(1, 16):
            pltpu.make_async_remote_copy(
                src_ref=part,
                dst_ref=part,
                send_sem=send1,
                recv_sem=recv1.at[c],
                device_id=(lax.rem(o + k, 16), g),
                device_id_type=MESH,
            ).start()

    for load in loads[2:]:
        load.wait()
    prepare(
        ids, weight_in, bias_in, buckets, gain1, weight_mid, bias_mid, gain2, weight_head,
        bias_head, u, we, wb, cols, off, end,
    )

    lane = iota((16, 128), 1)
    hot2 = None
    done = 0
    for c, (start, rows) in enumerate(CHUNKS):
        wait_for(got.at[pl.ds(0, 15), pl.ds(start, rows)], recv1.at[c])
        if c == 0:
            label = got[0, 0:1, :]
            for l in range(1, 16):
                label = jnp.maximum(label, got[l, 0:1, :])
            m = iota((16, 128), 0)
            pg, colour = m // 3, m % 3
            wanted = 6 * o + 6 * ((pg + 1) // 2 - 1) + 2 * colour + (pg + 1) % 2
            hot = jnp.where((label == wanted.astype(F32)) & (m < 12), 1.0, 0.0).astype(BF16)
            hot2 = jnp.concatenate([hot, hot], axis=1)
        for at in range(max(start - 1, 0) // 6, (start + rows - 1) // 6):
            pieces = []
            for l in range(16):
                pieces += [got[l, pl.ds(1 + 6 * at, 6), :], jnp.zeros((2, 128), F32)]
            hi, lo = halves(jnp.concatenate(pieces, axis=0))
            column = 128 * (PIECES[at] + 1)
            picked[:, column : column + 128] = dot(hot2, jnp.concatenate([hi, lo], axis=0))
        count = WINDOWS[c]
        for s in range(done, done + count):
            col = lane % 64 + (COLS * s - 4)
            keep = (col >= 0) & (col < W)
            pieces = []
            for h in range(2):
                first = 128 + h * W + COLS * s - 4
                at = first // 128 * 128
                turned = pltpu.roll(picked[:, at : at + 256], (h * 64 - (first - at)) % 256, 1)
                pieces.append(turned[:, 0:128])
            both = jnp.where(lane < 64, pieces[0], pieces[1])
            sent[s] = jnp.where(keep, both, 0.0)
        for k in range(count):
            s = done + lax.rem(g + k, count)

            @pl.when(s != g)
            def _():
                pltpu.make_async_remote_copy(
                    src_ref=sent.at[s, pl.ds(0, 12)],
                    dst_ref=video.at[g, pl.ds(0, 12)],
                    send_sem=send2,
                    recv_sem=recv2,
                    device_id=(o, s),
                    device_id_type=MESH,
                ).start()

        done += count
    own = pltpu.make_async_copy(sent.at[g, pl.ds(0, 12)], video.at[g, pl.ds(0, 12)], own_sem)
    own.start()
    own.wait()
    wait_for(video.at[pl.ds(0, 15), pl.ds(0, 12)], recv2)


def wait_for(ref, sem):
    pltpu.make_async_copy(ref, ref, sem).wait()


def encode_kernel(
    position, video, u, we, wb, cols, off, end,
    out, x3, entry, xs, sums, mixed, zs, turned,
):
    o, s = position()
    lane = iota((1, LANES), 1)
    c4, t = lane // 64, lane % 16
    col = COLS * s + 4 * (t - 1) + c4
    in_frame = jnp.where((col >= 0) & (col < W), 1.0, 0.0)
    low = iota((16, 128), 1) < 64

    low12 = iota((12, 128), 1) < 64
    lines = []
    for f in range(FRAMES):
        blocks = [video[4 * clip + f, 0:12, :] for clip in range(CLIPS)]
        flipped = [pltpu.roll(x, 64, 1) for x in blocks]
        first = [jnp.where(low12, blocks[c], flipped[c + 1]) for c in (0, 2)]
        second = [jnp.where(low12, flipped[c], blocks[c + 1]) for c in (0, 2)]
        wide = jnp.concatenate(
            [jnp.concatenate(first, axis=1), jnp.concatenate(second, axis=1)], axis=0
        )
        hi = wide.astype(BF16).astype(F32)
        lines += [hi, wide - hi]
    k = iota((LANES, LANES), 0)
    j = iota((LANES, LANES), 1)
    source = j % 64 // 16 * 64 + 4 * (j % 16) + j // 64
    permute = jnp.where(k == source, 1.0, 0.0).astype(BF16)
    placed = dot(jnp.concatenate(lines, axis=0).astype(BF16), permute)

    def wide_column(which, at):
        column = cols[which, pl.ds(at, 16), :]
        return jnp.concatenate([column, column], axis=1)

    def shifted(v0, v1, select):
        b10, b32 = pltpu.roll(v0, 64, 1), pltpu.roll(v1, 64, 1)
        b3s, b0s = pltpu.roll(v1, 65, 1), pltpu.roll(v0, 63, 1)
        left = jnp.where(select, b3s, b10)
        middle = jnp.where(select, b10, b32)
        right = jnp.where(select, b32, b0s)
        return left, middle, right

    for f in range(FRAMES):
        block = placed[48 * f : 48 * f + 48]
        v0, v1 = block[:, 0:128], block[:, 128:256]
        left, middle, right = shifted(v0, v1, iota((48, 128), 1) < 64)
        taps = []
        for a, b in ((left, middle), (v0, v1), (middle, right)):
            both = jnp.concatenate([a, b], axis=1)
            taps += [both, both[0:24]]
        taps.append(jnp.zeros((40, LANES), F32))
        x3[pl.ds(f * LANES, LANES), :] = jnp.concatenate(taps, axis=0).astype(BF16)

    def entry_of(f):
        first = max(0, f - 2)
        k0 = (2 - (f - first)) * LANES
        entry[f] = dot(we[:, k0:], x3[pl.ds(first * LANES, (f - first + 1) * LANES), :])
        inverse = []
        for re in range(6):
            total = jnp.zeros((8, LANES), F32)
            for c in range(0, CH, 8):
                value = entry[f, pl.ds(re * CH + c, 8), :] + off[pl.ds(c, 8), :]
                entry[f, pl.ds(re * CH + c, 8), :] = value
                total = total + value * value
            mean = jnp.sum(total, axis=0, keepdims=True) * (1 / CH)
            scale = lax.rsqrt(mean + EPSILON) * in_frame
            if re == 0:
                scale = scale * jnp.where(o > 0, 1.0, 0.0)
            if re == 5:
                scale = scale * jnp.where(o < N_DP - 1, 1.0, 0.0)
            inverse.append(scale)

        def group(i, _):
            at = i * 16
            gain = wide_column(0, at)
            act = []
            for re in range(6):
                v = entry[f, pl.ds(re * CH + at, 16), :] * inverse[re] * gain
                act.append(v + v * jnp.tanh(v))
            d0, d1, d2, d3, d4, d5 = act
            a, b = d4 - 4 * d2, d3 - 4 * d1
            c, e = d4 - d2, 2 * (d3 - d1)
            made = (4 * d0 - 5 * d2 + d4, a + b, a - b, c + e, c - e, 4 * d1 - 5 * d3 + d5)
            for w in range(6):
                v0, v1 = made[w][:, 0:128], made[w][:, 128:256]
                left, middle, right = shifted(v0, v1, low)
                his, los = zip(*[halves(x) for x in (left, middle, right, v0, v1)])
                for d, (p, q) in enumerate(((0, 1), (3, 4), (1, 2))):
                    for part, source in enumerate((his, los, his)):
                        rows = pl.ds((part * 3 + d) * CH + at, 16)
                        xs[f, w, rows, 0:128] = source[p]
                        xs[f, w, rows, 128:256] = source[q]
            return 0

        lax.fori_loop(0, CH // 16, group, 0, unroll=True)

    def middle_of(f):
        reach = min(3, FRAMES - f)

        def step(w, _):
            y = dot(u[w, 0 : reach * CH, :], xs[f, w])
            for later in range(reach):
                part = y[later * CH : (later + 1) * CH]
                if f == 0 or later == 2:
                    sums[f + later, w] = part
                else:
                    sums[f + later, w] = sums[f + later, w] + part
            return 0

        lax.fori_loop(0, 6, step, 0, unroll=True)

    def latent_of(f):
        def group(i, totals):
            at = i * 16
            bias = wide_column(1, at)
            y = [sums[f, w, pl.ds(at, 16), :] for w in range(6)]
            s12, d12, s34, d34 = y[1] + y[2], y[1] - y[2], y[3] + y[4], y[3] - y[4]
            made = (y[0] + s12 + s34, d12 + 2 * d34, s12 + 4 * s34, d12 + 8 * d34 + y[5])
            fresh = []
            for r in range(4):
                v = entry[f, pl.ds((r + 1) * CH + at, 16), :] + bias + made[r]
                mixed[f, r, pl.ds(at, 16), :] = v
                fresh.append(totals[r] + v * v)
            return tuple(fresh)

        zero = jnp.zeros((16, LANES), F32)
        totals = lax.fori_loop(0, CH // 16, group, (zero,) * 4, unroll=True)
        inverse = [
            lax.rsqrt(jnp.sum(x, axis=0, keepdims=True) * (1 / CH) + EPSILON) for x in totals
        ]
        side = pl.ds(f % 2 * 128, 128)

        def finish(i, _):
            at = i * 16
            gain = wide_column(2, at)
            act = []
            for r in range(4):
                v = mixed[f, r, pl.ds(at, 16), :] * inverse[r] * gain
                act.append(v + v * jnp.tanh(v))
            for r in range(2):
                for pair in range(2):
                    p0 = act[r][:, pair * 128 : pair * 128 + 128]
                    p1 = act[2 + r][:, pair * 128 : pair * 128 + 128]
                    even = jnp.where(low, p0, pltpu.roll(p1, 64, 1))
                    odd = jnp.where(low, pltpu.roll(p0, 64, 1), p1)
                    for c, x in ((2 * pair, even), (2 * pair + 1, odd)):
                        hi, lo = halves(x)
                        rows = pl.ds((c * 2 + r) * CH + at, 16)
                        zs[f // 2, 0, rows, side] = hi
                        zs[f // 2, 1, rows, side] = lo
            return 0

        lax.fori_loop(0, CH // 16, finish, 0, unroll=True)

    def tokens_of(f):
        both = dot(wb[...], zs[f // 2, 0])
        bias = jnp.concatenate([end[...], end[...]], axis=1)
        made = both[0:128] + both[128:256] + dot(wb[0:128], zs[f // 2, 1]) + bias
        turned[f // 2] = jnp.transpose(made)
        for side in range(2):
            for clip in range(CLIPS):
                for t in range(13):
                    rows = pl.ds(side * 128 + clip * 16 + t + 1, 2, stride=64)
                    out[clip * 4 + f - 1 + side, :, pl.ds(t * 128, 128)] = turned[f // 2, rows, :]

    entry_of(0)
    for f in range(FRAMES):
        if f + 1 < FRAMES:
            entry_of(f + 1)
        middle_of(f)
        latent_of(f)
        if f % 2:
            tokens_of(f)


def shape(dims, dtype):
    return jax.ShapeDtypeStruct(dims, dtype)


MADE = (
    shape((6, 3 * CH, MID_K), BF16),
    shape((6 * CH, 3 * LANES), BF16),
    shape((256, 8 * CH), BF16),
    shape((3, CH, 128), F32),
    shape((CH, LANES), F32),
    shape((128, 128), F32),
)
VMEM_BYTES = 60 * 2**20
VMEM = pl.BlockSpec(memory_space=pltpu.VMEM)
HBM = pl.BlockSpec(memory_space=pltpu.HBM)
ENCODE_SCRATCH = [
    pltpu.VMEM((FRAMES * LANES, LANES), BF16),
    pltpu.VMEM((FRAMES, 6 * CH, LANES), F32),
    pltpu.VMEM((FRAMES, 6, MID_K, LANES), BF16),
    pltpu.VMEM((FRAMES, 6, CH, LANES), F32),
    pltpu.VMEM((FRAMES, 4, CH, LANES), F32),
    pltpu.VMEM((2, 2, 8 * CH, LANES), BF16),
    pltpu.VMEM((2, LANES, 128), F32),
]


def whole_kernel(*refs):
    args, out, (made, exchange, encode) = refs[:12], refs[12], refs[13:]
    exchange_kernel(*args, *made, *exchange)
    encode_kernel(where_am_i, *made, out, *encode)
    got, _, sent, send1, _, send2 = exchange[13:19]
    wait_for(got.at[pl.ds(0, 15), pl.ds(0, 79)], send1)
    wait_for(sent.at[pl.ds(0, 15), pl.ds(0, 12)], send2)


def where_am_i():
    return lax.axis_index("dp"), lax.axis_index("seq")


def body(
    loaded, tile_rows, bucket_ids, in_weight, in_bias, bucket_bias, norm_gain, mid_weight,
    mid_bias, head_gain, head_weight, head_bias,
):
    def line(x):
        return x.reshape(1, -1)

    return pl.pallas_call(
        whole_kernel,
        out_shape=shape((NF, 2, TILE), F32),
        in_specs=[HBM] * 12,
        out_specs=VMEM,
        scratch_shapes=[
            [pltpu.VMEM((NF, 16, 128), F32)] + [pltpu.VMEM(x.shape, x.dtype) for x in MADE],
            [
                pltpu.VMEM((6, 1, TILE), F32),
                pltpu.SMEM((1, 6), I32),
                pltpu.SMEM((4,), I32),
                pltpu.VMEM((81, CH), F32),
                pltpu.VMEM((1, CH), F32),
                pltpu.VMEM((4, CH), F32),
                pltpu.VMEM((1, CH), F32),
                pltpu.VMEM((27, CH, CH), F32),
                pltpu.VMEM((1, CH), F32),
                pltpu.VMEM((1, CH), F32),
                pltpu.VMEM((ZCH, CH), F32),
                pltpu.VMEM((1, ZCH), F32),
                pltpu.SemaphoreType.DMA((12,)),
                pltpu.VMEM((16, 80, 128), F32),
                pltpu.VMEM((16, TILE + 256), F32),
                pltpu.VMEM((N_SEQ, 16, 128), F32),
                pltpu.SemaphoreType.DMA,
                pltpu.SemaphoreType.DMA((3,)),
                pltpu.SemaphoreType.DMA,
                pltpu.SemaphoreType.DMA,
                pltpu.SemaphoreType.DMA,
            ],
            ENCODE_SCRATCH,
        ],
        compiler_params=pltpu.CompilerParams(
            collective_id=0, has_side_effects=True, vmem_limit_bytes=VMEM_BYTES
        ),
    )(
        jnp.transpose(loaded, (1, 0, 2)), tile_rows, bucket_ids, in_weight.T, line(in_bias), bucket_bias, line(norm_gain),
        mid_weight, line(mid_bias), line(head_gain), head_weight, line(head_bias),
    )


def solution(mesh):
    return jax.shard_map(
        body,
        mesh=mesh,
        in_specs=(P("seq", "dp", None), P("seq", "dp")) + (P(),) * 10,
        out_specs=P(None, "dp", "seq"),
        check_vma=False,
    )
```

```python
import functools

import jax
import jax.numpy as jnp
from jax import lax
from jax.experimental import pallas as pl
from jax.experimental.pallas import tpu as pltpu
from jax.sharding import PartitionSpec as P

F32, BF16, I32 = jnp.float32, jnp.bfloat16, jnp.int32
MESH = pl.DeviceIdType.MESH
EPSILON = 1e-06
CH = 96
ZCH = 16
W = 832
NF = 16
FRAMES = 4
CLIPS = 4
N_DP = 16
N_SEQ = 16
COLS = W // N_SEQ
TILE = 2 * W
LANES = 256
MID_K = 9 * CH
PIECES = (0, 6, 7, 1, 8, 2, 9, 3, 10, 4, 11, 5, 12)
CHUNKS = ((0, 31), (31, 24), (55, 24))
WINDOWS = (4, 5, 7)


G43 = (
    (1 / 4, 0.0, 0.0),
    (-1 / 6, -1 / 6, -1 / 6),
    (-1 / 6, 1 / 6, -1 / 6),
    (1 / 24, 1 / 12, 1 / 6),
    (1 / 24, -1 / 12, 1 / 6),
    (0.0, 0.0, 1.0),
)


def iota(shape, dim):
    return lax.broadcasted_iota(I32, shape, dim)


def dot(a, b):
    return jnp.dot(a, b, preferred_element_type=F32)


def halves(x):
    hi = x.astype(BF16)
    return hi, (x - hi.astype(F32)).astype(BF16)


def prepare(
    ids, in_weight, in_bias, bucket_bias, norm_gain, mid_weight, mid_bias, head_gain,
    head_weight, head_bias, u, we, wb, cols, end,
):
    for a in range(3):
        for d in range(3):
            taps = [mid_weight[9 * a + 3 * b + d] for b in range(3)]
            outer, inner = taps[0] + taps[2], taps[1]
            s4 = taps[0] * (1 / 24) + taps[2] * (1 / 6)
            made = (
                taps[0] * 0.25,
                (outer + inner) * (-1 / 6),
                (inner - outer) * (1 / 6),
                s4 + inner * (1 / 12),
                s4 - inner * (1 / 12),
                taps[2],
            )
            for w in range(6):
                hi, lo = halves(made[w])
                rows = pl.ds((2 - a) * CH, CH)
                u[w, rows, pl.ds(d * CH, CH)] = hi
                u[w, rows, pl.ds((3 + d) * CH, CH)] = hi
                u[w, rows, pl.ds((6 + d) * CH, CH)] = lo
    n = iota((81, LANES), 1)
    d, part, h, m = n // 72, n % 72 // 24, n % 24 // 12, n % 12
    key = 3 * d + m % 3
    row = 2 * (m // 3) + h
    first = n < 216
    k = iota((81, LANES), 0)
    whi, wlo = halves(jnp.transpose(in_weight[...]))
    lines = jnp.concatenate(
        [in_bias[...], bucket_bias[...], norm_gain[...], mid_bias[...], head_gain[...]], axis=0
    )
    table = jnp.transpose(lines)
    lane = iota((CH, LANES), 1)
    offsets = jnp.zeros((CH, LANES), F32)
    for c in range(CLIPS):
        rest = table[:, 0:1] + sum(
            table[:, 1 + b : 2 + b] * jnp.where(ids[c] == b, 1.0, 0.0) for b in range(4)
        )
        for i in range(3):
            piece = rest.astype(BF16).astype(F32)
            offsets = jnp.where(lane == 216 + 3 * c + i, piece, offsets)
            rest = rest - piece
    for re in range(6):
        b = row - re
        legal = first & (b >= 0) & (b <= 2)
        for a in range(3):
            hit = legal & (k == 27 * a + 9 * b + key)
            e01 = jnp.where(hit & (part < 2), 1.0, 0.0).astype(BF16)
            e2 = jnp.where(hit & (part == 2), 1.0, 0.0).astype(BF16)
            got = dot(whi, e01) + dot(wlo, e2)
            if a == 2:
                got = got + offsets
            we[pl.ds(re * CH, CH), pl.ds(a * LANES, LANES)] = got.astype(BF16)
    for i, (at, scale) in enumerate(((5, 0.5), (6, 1.0), (7, 0.5))):
        cols[i] = jnp.broadcast_to(table[:, at : at + 1] * scale, (CH, 128))
    line = iota((128, ZCH), 0)
    spread = jnp.where(line % 64 // 4 == iota((128, ZCH), 1), 1.0, 0.0)
    hhi, hlo = halves(head_weight[...])
    line = iota((128, CH), 0)
    for part, piece in enumerate((hhi, hlo)):
        wide = dot(spread.astype(BF16), piece)
        for c4 in range(4):
            for r in range(2):
                q2, s = c4 // 2, c4 % 2
                keep = (line // 64 == q2) & (line % 2 == s) & (line % 4 // 2 == r)
                at = (c4 * 2 + r) * CH
                wb[pl.ds(part * 128, 128), pl.ds(at, CH)] = jnp.where(keep, wide, 0.0).astype(BF16)
    hb = jnp.sum(spread * head_bias[...], axis=1, keepdims=True)
    end[...] = jnp.broadcast_to(hb, (128, 128))


def exchange_kernel(
    loaded, tile_rows, bucket_ids, in_weight, in_bias, bucket_bias, norm_gain, mid_weight, mid_bias,
    head_gain, head_weight, head_bias,
    video, u, we, wb, cols, end,
    raw, numbers_smem, ids, weight_in, bias_in, buckets, gain1, weight_mid, bias_mid, gain2,
    weight_head, bias_head, in_sems,
    got, picked, sent, send1, recv1, send2, recv2, own_sem,
):
    o, g = lax.axis_index("dp"), lax.axis_index("seq")
    sources = (
        loaded, tile_rows, bucket_ids, in_weight, in_bias, bucket_bias, norm_gain, mid_weight,
        mid_bias, head_gain, head_weight, head_bias,
    )
    targets = (
        raw, numbers_smem, ids, weight_in, bias_in, buckets, gain1, weight_mid, bias_mid, gain2,
        weight_head, bias_head,
    )
    loads = [
        pltpu.make_async_copy(a, b, in_sems.at[i]) for i, (a, b) in enumerate(zip(sources, targets))
    ]
    for load in loads:
        load.start()
    barrier = pltpu.get_barrier_semaphore()
    for k in range(1, 16):
        pl.semaphore_signal(barrier, 1, device_id=(lax.rem(o + k, 16), g), device_id_type=MESH)
        pl.semaphore_signal(barrier, 1, device_id=(o, lax.rem(g + k, 16)), device_id_type=MESH)

    loads[0].wait()
    loads[1].wait()
    lane = iota((1, 128), 1)
    numbers = jnp.full((1, 128), -1000.0, F32)
    for j in range(6):
        numbers = jnp.where(lane == 8 * o + j, numbers_smem[0, j].astype(F32), numbers)
        for at, t in enumerate(PIECES):
            got[o, pl.ds(1 + 6 * at + j, 1), :] = raw[j, :, t * 128 : t * 128 + 128]
    got[o, 0:1, :] = numbers
    picked[:, 0:128] = jnp.zeros((16, 128), F32)
    picked[:, 128 + TILE :] = jnp.zeros((16, 128), F32)
    pl.semaphore_wait(barrier, 30)

    for c, (start, rows) in enumerate(CHUNKS):
        part = got.at[o, pl.ds(start, rows)]
        for k in range(1, 16):
            pltpu.make_async_remote_copy(
                src_ref=part,
                dst_ref=part,
                send_sem=send1,
                recv_sem=recv1.at[c],
                device_id=(lax.rem(o + k, 16), g),
                device_id_type=MESH,
            ).start()

    for load in loads[2:]:
        load.wait()
    prepare(
        ids, weight_in, bias_in, buckets, gain1, weight_mid, bias_mid, gain2, weight_head,
        bias_head, u, we, wb, cols, end,
    )

    lane = iota((16, 128), 1)
    hot2 = None
    done = 0
    for c, (start, rows) in enumerate(CHUNKS):
        wait_for(got.at[pl.ds(0, 15), pl.ds(start, rows)], recv1.at[c])
        if c == 0:
            label = got[0, 0:1, :]
            for l in range(1, 16):
                label = jnp.maximum(label, got[l, 0:1, :])
            m = iota((16, 128), 0)
            pg, colour = m // 3, m % 3
            wanted = 6 * o + 6 * ((pg + 1) // 2 - 1) + 2 * colour + (pg + 1) % 2
            hot = jnp.where((label == wanted.astype(F32)) & (m < 12), 1.0, 0.0).astype(BF16)
            hot2 = jnp.concatenate([hot, hot], axis=1)
        for at in range(max(start - 1, 0) // 6, (start + rows - 1) // 6):
            pieces = []
            for l in range(16):
                pieces += [got[l, pl.ds(1 + 6 * at, 6), :], jnp.zeros((2, 128), F32)]
            hi, lo = halves(jnp.concatenate(pieces, axis=0))
            column = 128 * (PIECES[at] + 1)
            picked[:, column : column + 128] = dot(hot2, jnp.concatenate([hi, lo], axis=0))
        count = WINDOWS[c]
        for s in range(done, done + count):
            col = lane % 64 + (COLS * s - 4)
            keep = (col >= 0) & (col < W)
            pieces = []
            for h in range(2):
                first = 128 + h * W + COLS * s - 4
                at = first // 128 * 128
                turned = pltpu.roll(picked[:, at : at + 256], (h * 64 - (first - at)) % 256, 1)
                pieces.append(turned[:, 0:128])
            both = jnp.where(lane < 64, pieces[0], pieces[1])
            sent[s] = jnp.where(keep, both, 0.0)
        for k in range(count):
            s = done + lax.rem(g + k, count)

            @pl.when(s != g)
            def _():
                pltpu.make_async_remote_copy(
                    src_ref=sent.at[s, pl.ds(0, 12)],
                    dst_ref=video.at[g, pl.ds(0, 12)],
                    send_sem=send2,
                    recv_sem=recv2,
                    device_id=(o, s),
                    device_id_type=MESH,
                ).start()

        done += count
    own = pltpu.make_async_copy(sent.at[g, pl.ds(0, 12)], video.at[g, pl.ds(0, 12)], own_sem)
    own.start()
    own.wait()
    wait_for(video.at[pl.ds(0, 15), pl.ds(0, 12)], recv2)


def wait_for(ref, sem):
    pltpu.make_async_copy(ref, ref, sem).wait()


def encode_kernel(
    position, video, u, we, wb, cols, end,
    out, x3, entry, xs, sums, mixed, zs, turned,
):
    o, s = position()
    lane = iota((1, LANES), 1)
    c4, t = lane // 64, lane % 16
    col = COLS * s + 4 * (t - 1) + c4
    in_frame = jnp.where((col >= 0) & (col < W), 1.0, 0.0)
    low = iota((16, 128), 1) < 64

    low12 = iota((12, 128), 1) < 64
    lines = []
    for f in range(FRAMES):
        blocks = [video[4 * clip + f, 0:12, :] for clip in range(CLIPS)]
        flipped = [pltpu.roll(x, 64, 1) for x in blocks]
        first = [jnp.where(low12, blocks[c], flipped[c + 1]) for c in (0, 2)]
        second = [jnp.where(low12, flipped[c], blocks[c + 1]) for c in (0, 2)]
        wide = jnp.concatenate(
            [jnp.concatenate(first, axis=1), jnp.concatenate(second, axis=1)], axis=0
        )
        hi = wide.astype(BF16).astype(F32)
        lines += [hi, wide - hi]
    k = iota((LANES, LANES), 0)
    j = iota((LANES, LANES), 1)
    source = j % 64 // 16 * 64 + 4 * (j % 16) + j // 64
    permute = jnp.where(k == source, 1.0, 0.0).astype(BF16)
    placed = dot(jnp.concatenate(lines, axis=0).astype(BF16), permute)

    def wide_column(which, at):
        column = cols[which, pl.ds(at, 16), :]
        return jnp.concatenate([column, column], axis=1)

    def shifted(v0, v1, select):
        b10, b32 = pltpu.roll(v0, 64, 1), pltpu.roll(v1, 64, 1)
        b3s, b0s = pltpu.roll(v1, 65, 1), pltpu.roll(v0, 63, 1)
        left = jnp.where(select, b3s, b10)
        middle = jnp.where(select, b10, b32)
        right = jnp.where(select, b32, b0s)
        return left, middle, right

    which_clip = jnp.where(
        iota((40, LANES), 0) // 3 == iota((40, LANES), 1) % 64 // 16, 1.0, 0.0
    )
    for f in range(FRAMES):
        block = placed[48 * f : 48 * f + 48]
        v0, v1 = block[:, 0:128], block[:, 128:256]
        left, middle, right = shifted(v0, v1, iota((48, 128), 1) < 64)
        taps = []
        for a, b in ((left, middle), (v0, v1), (middle, right)):
            both = jnp.concatenate([a, b], axis=1)
            taps += [both, both[0:24]]
        taps.append(which_clip)
        x3[pl.ds(f * LANES, LANES), :] = jnp.concatenate(taps, axis=0).astype(BF16)

    scales = {}

    def entry_dot(f):
        first = max(0, f - 2)
        k0 = (2 - (f - first)) * LANES
        entry[f] = dot(we[:, k0:], x3[pl.ds(first * LANES, (f - first + 1) * LANES), :])

    def entry_norm(f):
        inverse = []
        for re in range(6):
            total = jnp.zeros((8, LANES), F32)
            for c in range(0, CH, 8):
                value = entry[f, pl.ds(re * CH + c, 8), :]
                total = total + value * value
            mean = jnp.sum(total, axis=0, keepdims=True) * (1 / CH)
            scale = lax.rsqrt(mean + EPSILON) * in_frame
            if re == 0:
                scale = scale * jnp.where(o > 0, 1.0, 0.0)
            if re == 5:
                scale = scale * jnp.where(o < N_DP - 1, 1.0, 0.0)
            inverse.append(scale)
        scales[f] = inverse

    def active_of(f):
        def group(i):
            inverse = scales[f]
            at = i * 16
            gain = wide_column(0, at)
            act = []
            for re in range(6):
                v = entry[f, pl.ds(re * CH + at, 16), :] * inverse[re] * gain
                act.append(v + v * jnp.tanh(v))
            d0, d1, d2, d3, d4, d5 = act
            a, b = d4 - 4 * d2, d3 - 4 * d1
            c, e = d4 - d2, 2 * (d3 - d1)
            made = (4 * d0 - 5 * d2 + d4, a + b, a - b, c + e, c - e, 4 * d1 - 5 * d3 + d5)
            for w in range(6):
                v0, v1 = made[w][:, 0:128], made[w][:, 128:256]
                left, middle, right = shifted(v0, v1, low)
                his, los = zip(*[halves(x) for x in (left, middle, right, v0, v1)])
                for d, (p, q) in enumerate(((0, 1), (3, 4), (1, 2))):
                    for part, source in enumerate((his, los, his)):
                        rows = pl.ds((part * 3 + d) * CH + at, 16)
                        xs[f, w, rows, 0:128] = source[p]
                        xs[f, w, rows, 128:256] = source[q]

        return [functools.partial(group, i) for i in range(CH // 16)]

    def middle_of(f):
        reach = min(3, FRAMES - f)

        def step(w):
            y = dot(u[w, 0 : reach * CH, :], xs[f, w])
            for later in range(reach):
                part = y[later * CH : (later + 1) * CH]
                if f == 0 or later == 2:
                    sums[f + later, w] = part
                else:
                    sums[f + later, w] = sums[f + later, w] + part

        return [functools.partial(step, w) for w in range(6)]

    squares = {}

    def mixed_of(f):
        def group(i):
            at = i * 16
            bias = wide_column(1, at)
            y = [sums[f, w, pl.ds(at, 16), :] for w in range(6)]
            s12, d12, s34, d34 = y[1] + y[2], y[1] - y[2], y[3] + y[4], y[3] - y[4]
            made = (y[0] + s12 + s34, d12 + 2 * d34, s12 + 4 * s34, d12 + 8 * d34 + y[5])
            fresh = []
            for r in range(4):
                v = entry[f, pl.ds((r + 1) * CH + at, 16), :] + bias + made[r]
                mixed[f, r, pl.ds(at, 16), :] = v
                fresh.append(v * v + squares[f][r] if i else v * v)
            squares[f] = fresh

        return [functools.partial(group, i) for i in range(CH // 16)]

    def latent_of(f):
        side = pl.ds(f % 2 * 128, 128)

        def group(i):
            if i == 0:
                squares[f] = [
                    lax.rsqrt(jnp.sum(x, axis=0, keepdims=True) * (1 / CH) + EPSILON)
                    for x in squares[f]
                ]
            inverse = squares[f]
            at = i * 16
            gain = wide_column(2, at)
            act = []
            for r in range(4):
                v = mixed[f, r, pl.ds(at, 16), :] * inverse[r] * gain
                act.append(v + v * jnp.tanh(v))
            for r in range(2):
                for pair in range(2):
                    p0 = act[r][:, pair * 128 : pair * 128 + 128]
                    p1 = act[2 + r][:, pair * 128 : pair * 128 + 128]
                    even = jnp.where(low, p0, pltpu.roll(p1, 64, 1))
                    odd = jnp.where(low, pltpu.roll(p0, 64, 1), p1)
                    for c, x in ((2 * pair, even), (2 * pair + 1, odd)):
                        hi, lo = halves(x)
                        rows = pl.ds((c * 2 + r) * CH + at, 16)
                        zs[f // 2, 0, rows, side] = hi
                        zs[f // 2, 1, rows, side] = lo

        return [functools.partial(group, i) for i in range(CH // 16)]

    def tokens_of(f):
        both = dot(wb[...], zs[f // 2, 0])
        bias = jnp.concatenate([end[...], end[...]], axis=1)
        made = both[0:128] + both[128:256] + dot(wb[0:128], zs[f // 2, 1]) + bias
        turned[f // 2] = jnp.transpose(made)
        for side in range(2):
            for clip in range(CLIPS):
                for t in range(13):
                    rows = pl.ds(side * 128 + clip * 16 + t + 1, 2, stride=64)
                    out[clip * 4 + f - 1 + side, :, pl.ds(t * 128, 128)] = turned[f // 2, rows, :]

    def beside(main, *others):
        rest = [task for tasks in others for task in tasks]
        for i, task in enumerate(main):
            task()
            for other in rest[i * len(rest) // len(main) : (i + 1) * len(rest) // len(main)]:
                other()

    def run(f, task):
        return [functools.partial(task, f)]

    entry_dot(0)
    entry_dot(1)
    entry_norm(0)
    beside(active_of(0), run(2, entry_dot), run(1, entry_norm))
    beside(middle_of(0), active_of(1), run(3, entry_dot), run(2, entry_norm))
    beside(middle_of(1), active_of(2), mixed_of(0), latent_of(0), run(3, entry_norm))
    beside(middle_of(2), active_of(3), mixed_of(1), latent_of(1))
    beside(middle_of(3), run(1, tokens_of), mixed_of(2), latent_of(2))
    for tasks in (mixed_of(3), latent_of(3)):
        for task in tasks:
            task()
    tokens_of(3)


def shape(dims, dtype):
    return jax.ShapeDtypeStruct(dims, dtype)


MADE = (
    shape((6, 3 * CH, MID_K), BF16),
    shape((6 * CH, 3 * LANES), BF16),
    shape((256, 8 * CH), BF16),
    shape((3, CH, 128), F32),
    shape((128, 128), F32),
)
VMEM_BYTES = 48 * 2**20
VMEM = pl.BlockSpec(memory_space=pltpu.VMEM)
HBM = pl.BlockSpec(memory_space=pltpu.HBM)
ENCODE_SCRATCH = [
    pltpu.VMEM((FRAMES * LANES, LANES), BF16),
    pltpu.VMEM((FRAMES, 6 * CH, LANES), F32),
    pltpu.VMEM((FRAMES, 6, MID_K, LANES), BF16),
    pltpu.VMEM((FRAMES, 6, CH, LANES), F32),
    pltpu.VMEM((FRAMES, 4, CH, LANES), F32),
    pltpu.VMEM((2, 2, 8 * CH, LANES), BF16),
    pltpu.VMEM((2, LANES, 128), F32),
]


def whole_kernel(*refs):
    args, out, (made, exchange, encode) = refs[:12], refs[12], refs[13:]
    exchange_kernel(*args, *made, *exchange)
    encode_kernel(where_am_i, *made, out, *encode)
    got, _, sent, send1, _, send2 = exchange[13:19]
    wait_for(got.at[pl.ds(0, 15), pl.ds(0, 79)], send1)
    wait_for(sent.at[pl.ds(0, 15), pl.ds(0, 12)], send2)


def where_am_i():
    return lax.axis_index("dp"), lax.axis_index("seq")


def body(
    loaded, tile_rows, bucket_ids, in_weight, in_bias, bucket_bias, norm_gain, mid_weight,
    mid_bias, head_gain, head_weight, head_bias,
):
    def line(x):
        return x.reshape(1, -1)

    operands = (
        jnp.transpose(loaded, (1, 0, 2)), tile_rows, bucket_ids, in_weight.T, line(in_bias),
        bucket_bias, line(norm_gain), mid_weight, line(mid_bias), line(head_gain), head_weight,
        line(head_bias),
    )
    return pl.pallas_call(
        whole_kernel,
        out_shape=pltpu.VMEM((NF, 2, TILE), F32),
        in_specs=[HBM] * 12,
        out_specs=VMEM,
        scratch_shapes=[
            [pltpu.VMEM((NF, 16, 128), F32)] + [pltpu.VMEM(x.shape, x.dtype) for x in MADE],
            [
                pltpu.VMEM((6, 1, TILE), F32),
                pltpu.SMEM((1, 6), I32),
                pltpu.SMEM((4,), I32),
                pltpu.VMEM((81, CH), F32),
                pltpu.VMEM((1, CH), F32),
                pltpu.VMEM((4, CH), F32),
                pltpu.VMEM((1, CH), F32),
                pltpu.VMEM((27, CH, CH), F32),
                pltpu.VMEM((1, CH), F32),
                pltpu.VMEM((1, CH), F32),
                pltpu.VMEM((ZCH, CH), F32),
                pltpu.VMEM((1, ZCH), F32),
                pltpu.SemaphoreType.DMA((12,)),
                pltpu.VMEM((16, 80, 128), F32),
                pltpu.VMEM((16, TILE + 256), F32),
                pltpu.VMEM((N_SEQ, 16, 128), F32),
                pltpu.SemaphoreType.DMA,
                pltpu.SemaphoreType.DMA((3,)),
                pltpu.SemaphoreType.DMA,
                pltpu.SemaphoreType.DMA,
                pltpu.SemaphoreType.DMA,
            ],
            ENCODE_SCRATCH,
        ],
        compiler_params=pltpu.CompilerParams(
            collective_id=0, has_side_effects=True, vmem_limit_bytes=VMEM_BYTES
        ),
    )(*[pltpu.with_memory_space_constraint(x, pltpu.HBM) for x in operands])


def solution(mesh):
    return jax.shard_map(
        body,
        mesh=mesh,
        in_specs=(P("seq", "dp", None), P("seq", "dp")) + (P(),) * 10,
        out_specs=P(None, "dp", "seq"),
        check_vma=False,
    )
```

```python
import functools

import jax
import jax.numpy as jnp
from jax import lax
from jax.experimental import pallas as pl
from jax.experimental.pallas import tpu as pltpu
from jax.sharding import PartitionSpec as P

F32, BF16, I32 = jnp.float32, jnp.bfloat16, jnp.int32
MESH = pl.DeviceIdType.MESH
EPSILON = 1e-06
CH = 96
ZCH = 16
W = 832
NF = 16
FRAMES = 4
CLIPS = 4
N_DP = 16
N_SEQ = 16
COLS = W // N_SEQ
TILE = 2 * W
LANES = 256
MID_K = 9 * CH
PIECES = (0, 6, 7, 1, 8, 2, 9, 3, 10, 4, 11, 5, 12)
CHUNKS = ((0, 31), (31, 24), (55, 24))
WINDOWS = (4, 5, 7)


G43 = (
    (1 / 4, 0.0, 0.0),
    (-1 / 6, -1 / 6, -1 / 6),
    (-1 / 6, 1 / 6, -1 / 6),
    (1 / 24, 1 / 12, 1 / 6),
    (1 / 24, -1 / 12, 1 / 6),
    (0.0, 0.0, 1.0),
)


def iota(shape, dim):
    return lax.broadcasted_iota(I32, shape, dim)


def dot(a, b):
    return jnp.dot(a, b, preferred_element_type=F32)


def halves(x):
    hi = x.astype(BF16)
    return hi, (x - hi.astype(F32)).astype(BF16)


def prepare(
    ids, in_weight, in_bias, bucket_bias, norm_gain, mid_weight, mid_bias, head_gain,
    head_weight, head_bias, u, we, wb, cols, end,
):
    for a in range(3):
        for d in range(3):
            taps = [mid_weight[9 * a + 3 * b + d] for b in range(3)]
            outer, inner = taps[0] + taps[2], taps[1]
            s4 = taps[0] * (1 / 24) + taps[2] * (1 / 6)
            made = (
                taps[0] * 0.25,
                (outer + inner) * (-1 / 6),
                (inner - outer) * (1 / 6),
                s4 + inner * (1 / 12),
                s4 - inner * (1 / 12),
                taps[2],
            )
            for w in range(6):
                hi, lo = halves(made[w])
                rows = pl.ds((2 - a) * CH, CH)
                u[w, rows, pl.ds(d * CH, CH)] = hi
                u[w, rows, pl.ds((3 + d) * CH, CH)] = hi
                u[w, rows, pl.ds((6 + d) * CH, CH)] = lo
    n = iota((81, LANES), 1)
    d, part, h, m = n // 72, n % 72 // 24, n % 24 // 12, n % 12
    key = 3 * d + m % 3
    row = 2 * (m // 3) + h
    first = n < 216
    k = iota((81, LANES), 0)
    whi, wlo = halves(jnp.transpose(in_weight[...]))
    lines = jnp.concatenate(
        [in_bias[...], bucket_bias[...], norm_gain[...], mid_bias[...], head_gain[...]], axis=0
    )
    table = jnp.transpose(lines)
    lane = iota((CH, LANES), 1)
    offsets = jnp.zeros((CH, LANES), F32)
    for c in range(CLIPS):
        rest = table[:, 0:1] + sum(
            table[:, 1 + b : 2 + b] * jnp.where(ids[c] == b, 1.0, 0.0) for b in range(4)
        )
        for i in range(3):
            piece = rest.astype(BF16).astype(F32)
            offsets = jnp.where(lane == 216 + 3 * c + i, piece, offsets)
            rest = rest - piece
    for re in range(6):
        b = row - re
        legal = first & (b >= 0) & (b <= 2)
        for a in range(3):
            hit = legal & (k == 27 * a + 9 * b + key)
            e01 = jnp.where(hit & (part < 2), 1.0, 0.0).astype(BF16)
            e2 = jnp.where(hit & (part == 2), 1.0, 0.0).astype(BF16)
            got = dot(whi, e01) + dot(wlo, e2)
            if a == 2:
                got = got + offsets
            we[pl.ds(re * CH, CH), pl.ds(a * LANES, LANES)] = got.astype(BF16)
    for i, (at, scale) in enumerate(((5, 0.5), (6, 1.0), (7, 0.5))):
        cols[i] = jnp.broadcast_to(table[:, at : at + 1] * scale, (CH, 128))
    line = iota((128, ZCH), 0)
    spread = jnp.where(line % 64 // 4 == iota((128, ZCH), 1), 1.0, 0.0)
    hhi, hlo = halves(head_weight[...])
    line = iota((128, CH), 0)
    for part, piece in enumerate((hhi, hlo)):
        wide = dot(spread.astype(BF16), piece)
        for c4 in range(4):
            for r in range(2):
                q2, s = c4 // 2, c4 % 2
                keep = (line // 64 == q2) & (line % 2 == s) & (line % 4 // 2 == r)
                at = (c4 * 2 + r) * CH
                wb[pl.ds(part * 128, 128), pl.ds(at, CH)] = jnp.where(keep, wide, 0.0).astype(BF16)
    hb = jnp.sum(spread * head_bias[...], axis=1, keepdims=True)
    end[...] = jnp.broadcast_to(hb, (128, 128))


def exchange_kernel(
    loaded, tile_rows, bucket_ids, in_weight, in_bias, bucket_bias, norm_gain, mid_weight, mid_bias,
    head_gain, head_weight, head_bias,
    video, u, we, wb, cols, end,
    raw, numbers_smem, ids, weight_in, bias_in, buckets, gain1, weight_mid, bias_mid, gain2,
    weight_head, bias_head, in_sems,
    got, picked, sent, send1, recv1, send2, recv2, own_sem,
):
    o, g = lax.axis_index("dp"), lax.axis_index("seq")
    barrier = pltpu.get_barrier_semaphore()
    for k in range(1, 16):
        pl.semaphore_signal(barrier, 1, device_id=(lax.rem(o + k, 16), g), device_id_type=MESH)
        pl.semaphore_signal(barrier, 1, device_id=(o, lax.rem(g + k, 16)), device_id_type=MESH)
    sources = (
        loaded, tile_rows, bucket_ids, in_weight, in_bias, bucket_bias, norm_gain, mid_weight,
        mid_bias, head_gain, head_weight, head_bias,
    )
    targets = (
        raw, numbers_smem, ids, weight_in, bias_in, buckets, gain1, weight_mid, bias_mid, gain2,
        weight_head, bias_head,
    )
    loads = [
        pltpu.make_async_copy(a, b, in_sems.at[i]) for i, (a, b) in enumerate(zip(sources, targets))
    ]
    for load in loads:
        load.start()
    loads[0].wait()
    loads[1].wait()
    lane = iota((1, 128), 1)
    numbers = jnp.full((1, 128), -1000.0, F32)
    for j in range(6):
        numbers = jnp.where(lane == 8 * o + j, numbers_smem[0, j].astype(F32), numbers)
        for at, t in enumerate(PIECES):
            got[o, pl.ds(1 + 6 * at + j, 1), :] = raw[j, :, t * 128 : t * 128 + 128]
    got[o, 0:1, :] = numbers
    picked[:, 0:128] = jnp.zeros((16, 128), F32)
    picked[:, 128 + TILE :] = jnp.zeros((16, 128), F32)
    pl.semaphore_wait(barrier, 30)

    for c, (start, rows) in enumerate(CHUNKS):
        part = got.at[o, pl.ds(start, rows)]
        for k in range(1, 16):
            pltpu.make_async_remote_copy(
                src_ref=part,
                dst_ref=part,
                send_sem=send1,
                recv_sem=recv1.at[c],
                device_id=(lax.rem(o + k, 16), g),
                device_id_type=MESH,
            ).start()

    for load in loads[2:]:
        load.wait()
    prepare(
        ids, weight_in, bias_in, buckets, gain1, weight_mid, bias_mid, gain2, weight_head,
        bias_head, u, we, wb, cols, end,
    )

    lane = iota((16, 128), 1)
    hot2 = None
    done = 0
    for c, (start, rows) in enumerate(CHUNKS):
        wait_for(got.at[pl.ds(0, 15), pl.ds(start, rows)], recv1.at[c])
        if c == 0:
            label = got[0, 0:1, :]
            for l in range(1, 16):
                label = jnp.maximum(label, got[l, 0:1, :])
            m = iota((16, 128), 0)
            pg, colour = m // 3, m % 3
            wanted = 6 * o + 6 * ((pg + 1) // 2 - 1) + 2 * colour + (pg + 1) % 2
            hot = jnp.where((label == wanted.astype(F32)) & (m < 12), 1.0, 0.0).astype(BF16)
            hot2 = jnp.concatenate([hot, hot], axis=1)
        for at in range(max(start - 1, 0) // 6, (start + rows - 1) // 6):
            pieces = []
            for l in range(16):
                pieces += [got[l, pl.ds(1 + 6 * at, 6), :], jnp.zeros((2, 128), F32)]
            hi, lo = halves(jnp.concatenate(pieces, axis=0))
            column = 128 * (PIECES[at] + 1)
            picked[:, column : column + 128] = dot(hot2, jnp.concatenate([hi, lo], axis=0))
        count = WINDOWS[c]
        for s in range(done, done + count):
            col = lane % 64 + (COLS * s - 4)
            keep = (col >= 0) & (col < W)
            pieces = []
            for h in range(2):
                first = 128 + h * W + COLS * s - 4
                at = first // 128 * 128
                turned = pltpu.roll(picked[:, at : at + 256], (h * 64 - (first - at)) % 256, 1)
                pieces.append(turned[:, 0:128])
            both = jnp.where(lane < 64, pieces[0], pieces[1])
            sent[s] = jnp.where(keep, both, 0.0)
        for k in range(count):
            s = done + lax.rem(g + k, count)

            @pl.when(s != g)
            def _():
                pltpu.make_async_remote_copy(
                    src_ref=sent.at[s, pl.ds(0, 12)],
                    dst_ref=video.at[g, pl.ds(0, 12)],
                    send_sem=send2,
                    recv_sem=recv2,
                    device_id=(o, s),
                    device_id_type=MESH,
                ).start()

        done += count
    own = pltpu.make_async_copy(sent.at[g, pl.ds(0, 12)], video.at[g, pl.ds(0, 12)], own_sem)
    own.start()
    own.wait()
    wait_for(video.at[pl.ds(0, 15), pl.ds(0, 12)], recv2)


def wait_for(ref, sem):
    pltpu.make_async_copy(ref, ref, sem).wait()


def encode_kernel(
    position, video, u, we, wb, cols, end,
    out, x3, entry, xs, sums, mixed, zs, turned,
):
    o, s = position()
    lane = iota((1, LANES), 1)
    c4, t = lane // 64, lane % 16
    col = COLS * s + 4 * (t - 1) + c4
    in_frame = jnp.where((col >= 0) & (col < W), 1.0, 0.0)
    low = iota((16, 128), 1) < 64

    low12 = iota((12, 128), 1) < 64
    k = iota((LANES, LANES), 0)
    j = iota((LANES, LANES), 1)
    source = j % 64 // 16 * 64 + 4 * (j % 16) + j // 64
    permute = jnp.where(k == source, 1.0, 0.0).astype(BF16)
    which_clip = jnp.where(
        iota((40, LANES), 0) // 3 == iota((40, LANES), 1) % 64 // 16, 1.0, 0.0
    )

    def pixels_of(f):
        blocks = [video[4 * clip + f, 0:12, :] for clip in range(CLIPS)]
        flipped = [pltpu.roll(x, 64, 1) for x in blocks]
        first = [jnp.where(low12, blocks[c], flipped[c + 1]) for c in (0, 2)]
        second = [jnp.where(low12, flipped[c], blocks[c + 1]) for c in (0, 2)]
        wide = jnp.concatenate(
            [jnp.concatenate(first, axis=1), jnp.concatenate(second, axis=1)], axis=0
        )
        hi = wide.astype(BF16).astype(F32)
        block = dot(jnp.concatenate([hi, wide - hi], axis=0).astype(BF16), permute)
        v0, v1 = block[:, 0:128], block[:, 128:256]
        left, middle, right = shifted(v0, v1, iota((48, 128), 1) < 64)
        taps = []
        for a, b in ((left, middle), (v0, v1), (middle, right)):
            both = jnp.concatenate([a, b], axis=1)
            taps += [both, both[0:24]]
        taps.append(which_clip)
        x3[pl.ds(f * LANES, LANES), :] = jnp.concatenate(taps, axis=0).astype(BF16)

    def wide_column(which, at):
        column = cols[which, pl.ds(at, 16), :]
        return jnp.concatenate([column, column], axis=1)

    def shifted(v0, v1, select):
        b10, b32 = pltpu.roll(v0, 64, 1), pltpu.roll(v1, 64, 1)
        b3s, b0s = pltpu.roll(v1, 65, 1), pltpu.roll(v0, 63, 1)
        left = jnp.where(select, b3s, b10)
        middle = jnp.where(select, b10, b32)
        right = jnp.where(select, b32, b0s)
        return left, middle, right

    scales = {}

    def entry_dot(f):
        first = max(0, f - 2)
        k0 = (2 - (f - first)) * LANES
        entry[f] = dot(we[:, k0:], x3[pl.ds(first * LANES, (f - first + 1) * LANES), :])

    def entry_norm(f):
        inverse = []
        for re in range(6):
            total = jnp.zeros((8, LANES), F32)
            for c in range(0, CH, 8):
                value = entry[f, pl.ds(re * CH + c, 8), :]
                total = total + value * value
            mean = jnp.sum(total, axis=0, keepdims=True) * (1 / CH)
            scale = lax.rsqrt(mean + EPSILON) * in_frame
            if re == 0:
                scale = scale * jnp.where(o > 0, 1.0, 0.0)
            if re == 5:
                scale = scale * jnp.where(o < N_DP - 1, 1.0, 0.0)
            inverse.append(scale)
        scales[f] = inverse

    def active_of(f):
        def group(i):
            inverse = scales[f]
            at = i * 16
            gain = wide_column(0, at)
            act = []
            for re in range(6):
                v = entry[f, pl.ds(re * CH + at, 16), :] * inverse[re] * gain
                act.append(v + v * jnp.tanh(v))
            d0, d1, d2, d3, d4, d5 = act
            a, b = d4 - 4 * d2, d3 - 4 * d1
            c, e = d4 - d2, 2 * (d3 - d1)
            made = (4 * d0 - 5 * d2 + d4, a + b, a - b, c + e, c - e, 4 * d1 - 5 * d3 + d5)
            for w in range(6):
                v0, v1 = made[w][:, 0:128], made[w][:, 128:256]
                left, middle, right = shifted(v0, v1, low)
                his, los = zip(*[halves(x) for x in (left, middle, right, v0, v1)])
                for d, (p, q) in enumerate(((0, 1), (3, 4), (1, 2))):
                    for part, source in enumerate((his, los, his)):
                        rows = pl.ds((part * 3 + d) * CH + at, 16)
                        xs[f, w, rows, 0:128] = source[p]
                        xs[f, w, rows, 128:256] = source[q]

        return [functools.partial(group, i) for i in range(CH // 16)]

    def middle_of(f):
        reach = min(3, FRAMES - f)

        def step(w):
            y = dot(u[w, 0 : reach * CH, :], xs[f, w])
            for later in range(reach):
                part = y[later * CH : (later + 1) * CH]
                if f == 0 or later == 2:
                    sums[f + later, w] = part
                else:
                    sums[f + later, w] = sums[f + later, w] + part

        return [functools.partial(step, w) for w in range(6)]

    squares = {}

    def mixed_of(f):
        def group(i):
            at = i * 16
            bias = wide_column(1, at)
            y = [sums[f, w, pl.ds(at, 16), :] for w in range(6)]
            s12, d12, s34, d34 = y[1] + y[2], y[1] - y[2], y[3] + y[4], y[3] - y[4]
            made = (y[0] + s12 + s34, d12 + 2 * d34, s12 + 4 * s34, d12 + 8 * d34 + y[5])
            fresh = []
            for r in range(4):
                v = entry[f, pl.ds((r + 1) * CH + at, 16), :] + bias + made[r]
                mixed[f, r, pl.ds(at, 16), :] = v
                fresh.append(v * v + squares[f][r] if i else v * v)
            squares[f] = fresh

        return [functools.partial(group, i) for i in range(CH // 16)]

    def latent_of(f):
        side = pl.ds(f % 2 * 128, 128)

        def group(i):
            if i == 0:
                squares[f] = [
                    lax.rsqrt(jnp.sum(x, axis=0, keepdims=True) * (1 / CH) + EPSILON)
                    for x in squares[f]
                ]
            inverse = squares[f]
            at = i * 16
            gain = wide_column(2, at)
            act = []
            for r in range(4):
                v = mixed[f, r, pl.ds(at, 16), :] * inverse[r] * gain
                act.append(v + v * jnp.tanh(v))
            for r in range(2):
                for pair in range(2):
                    p0 = act[r][:, pair * 128 : pair * 128 + 128]
                    p1 = act[2 + r][:, pair * 128 : pair * 128 + 128]
                    even = jnp.where(low, p0, pltpu.roll(p1, 64, 1))
                    odd = jnp.where(low, pltpu.roll(p0, 64, 1), p1)
                    for c, x in ((2 * pair, even), (2 * pair + 1, odd)):
                        hi, lo = halves(x)
                        rows = pl.ds((c * 2 + r) * CH + at, 16)
                        zs[f // 2, 0, rows, side] = hi
                        zs[f // 2, 1, rows, side] = lo

        return [functools.partial(group, i) for i in range(CH // 16)]

    def tokens_of(first, count):
        lanes = pl.ds(first % 2 * 128, count * 128)
        part = [zs[first // 2, i, :, lanes] for i in range(2)]
        both = dot(wb[...], part[0])
        bias = jnp.concatenate([end[...]] * count, axis=1)
        made = both[0:128] + both[128:256] + dot(wb[0:128], part[1]) + bias
        turned[first // 2, lanes, :] = jnp.transpose(made)
        for f in range(first, first + count):
            for clip in range(CLIPS):
                for t in range(13):
                    rows = pl.ds(f % 2 * 128 + clip * 16 + t + 1, 2, stride=64)
                    out[clip * 4 + f, :, pl.ds(t * 128, 128)] = turned[first // 2, rows, :]

    def beside(main, *others):
        rest = [task for tasks in others for task in tasks]
        for i, task in enumerate(main):
            task()
            for other in rest[i * len(rest) // len(main) : (i + 1) * len(rest) // len(main)]:
                other()

    def run(f, task):
        return [functools.partial(task, f)]

    pixels_of(0)
    entry_dot(0)
    pixels_of(1)
    entry_dot(1)
    entry_norm(0)
    pixels_of(2)
    pixels_of(3)
    beside(active_of(0), run(2, entry_dot), run(3, entry_dot), run(1, entry_norm))
    beside(middle_of(0), active_of(1), run(2, entry_norm))
    beside(middle_of(1), active_of(2), mixed_of(0), latent_of(0), run(3, entry_norm))
    beside(middle_of(2), active_of(3), mixed_of(1), latent_of(1))
    beside(middle_of(3), mixed_of(2), latent_of(2), [functools.partial(tokens_of, 0, 2)])
    tokens_of(2, 1)
    for tasks in (mixed_of(3), latent_of(3)):
        for task in tasks:
            task()
    tokens_of(3, 1)


def shape(dims, dtype):
    return jax.ShapeDtypeStruct(dims, dtype)


MADE = (
    shape((6, 3 * CH, MID_K), BF16),
    shape((6 * CH, 3 * LANES), BF16),
    shape((256, 8 * CH), BF16),
    shape((3, CH, 128), F32),
    shape((128, 128), F32),
)
VMEM_BYTES = 48 * 2**20
VMEM = pl.BlockSpec(memory_space=pltpu.VMEM)
HBM = pl.BlockSpec(memory_space=pltpu.HBM)
ENCODE_SCRATCH = [
    pltpu.VMEM((FRAMES * LANES, LANES), BF16),
    pltpu.VMEM((FRAMES, 6 * CH, LANES), F32),
    pltpu.VMEM((FRAMES, 6, MID_K, LANES), BF16),
    pltpu.VMEM((FRAMES, 6, CH, LANES), F32),
    pltpu.VMEM((FRAMES, 4, CH, LANES), F32),
    pltpu.VMEM((2, 2, 8 * CH, LANES), BF16),
    pltpu.VMEM((2, LANES, 128), F32),
]


def whole_kernel(*refs):
    args, out, (made, exchange, encode) = refs[:12], refs[12], refs[13:]
    exchange_kernel(*args, *made, *exchange)
    encode_kernel(where_am_i, *made, out, *encode)
    got, _, sent, send1, _, send2 = exchange[13:19]
    wait_for(got.at[pl.ds(0, 15), pl.ds(0, 79)], send1)
    wait_for(sent.at[pl.ds(0, 15), pl.ds(0, 12)], send2)


def where_am_i():
    return lax.axis_index("dp"), lax.axis_index("seq")


def body(
    loaded, tile_rows, bucket_ids, in_weight, in_bias, bucket_bias, norm_gain, mid_weight,
    mid_bias, head_gain, head_weight, head_bias,
):
    def line(x):
        return x.reshape(1, -1)

    operands = (
        jnp.transpose(loaded, (1, 0, 2)), tile_rows, bucket_ids, in_weight.T, line(in_bias),
        bucket_bias, line(norm_gain), mid_weight, line(mid_bias), line(head_gain), head_weight,
        line(head_bias),
    )
    return pl.pallas_call(
        whole_kernel,
        out_shape=pltpu.VMEM((NF, 2, TILE), F32),
        in_specs=[HBM] * 12,
        out_specs=VMEM,
        scratch_shapes=[
            [pltpu.VMEM((NF, 16, 128), F32)] + [pltpu.VMEM(x.shape, x.dtype) for x in MADE],
            [
                pltpu.VMEM((6, 1, TILE), F32),
                pltpu.SMEM((1, 6), I32),
                pltpu.SMEM((4,), I32),
                pltpu.VMEM((81, CH), F32),
                pltpu.VMEM((1, CH), F32),
                pltpu.VMEM((4, CH), F32),
                pltpu.VMEM((1, CH), F32),
                pltpu.VMEM((27, CH, CH), F32),
                pltpu.VMEM((1, CH), F32),
                pltpu.VMEM((1, CH), F32),
                pltpu.VMEM((ZCH, CH), F32),
                pltpu.VMEM((1, ZCH), F32),
                pltpu.SemaphoreType.DMA((12,)),
                pltpu.VMEM((16, 80, 128), F32),
                pltpu.VMEM((16, TILE + 256), F32),
                pltpu.VMEM((N_SEQ, 16, 128), F32),
                pltpu.SemaphoreType.DMA,
                pltpu.SemaphoreType.DMA((3,)),
                pltpu.SemaphoreType.DMA,
                pltpu.SemaphoreType.DMA,
                pltpu.SemaphoreType.DMA,
            ],
            ENCODE_SCRATCH,
        ],
        compiler_params=pltpu.CompilerParams(
            collective_id=0, has_side_effects=True, vmem_limit_bytes=VMEM_BYTES
        ),
    )(*[pltpu.with_memory_space_constraint(x, pltpu.HBM) for x in operands])


def solution(mesh):
    return jax.shard_map(
        body,
        mesh=mesh,
        in_specs=(P("seq", "dp", None), P("seq", "dp")) + (P(),) * 10,
        out_specs=P(None, "dp", "seq"),
        check_vma=False,
    )
```

```python
import functools

import jax
import jax.numpy as jnp
from jax import lax
from jax.experimental import pallas as pl
from jax.experimental.pallas import tpu as pltpu
from jax.sharding import PartitionSpec as P

F32, BF16, I32 = jnp.float32, jnp.bfloat16, jnp.int32
MESH = pl.DeviceIdType.MESH
EPSILON = 1e-06
CH = 96
ZCH = 16
W = 832
NF = 16
FRAMES = 4
CLIPS = 4
N_DP = 16
N_SEQ = 16
COLS = W // N_SEQ
TILE = 2 * W
LANES = 256
MID_K = 9 * CH
PIECES = (0, 6, 7, 1, 8, 2, 9, 3, 10, 4, 11, 5, 12)
CHUNKS = ((0, 31), (31, 24), (55, 24))
WINDOWS = (4, 5, 7)
FAR_SEQ = (8, 9, 7, 6, 10, 5, 11, 4, 12, 3, 13, 2, 14, 1, 15)
FAR_DP = (10, 6, 9, 11, 14, 2, 8, 5, 7, 13, 15, 1, 3, 4, 12)


G43 = (
    (1 / 4, 0.0, 0.0),
    (-1 / 6, -1 / 6, -1 / 6),
    (-1 / 6, 1 / 6, -1 / 6),
    (1 / 24, 1 / 12, 1 / 6),
    (1 / 24, -1 / 12, 1 / 6),
    (0.0, 0.0, 1.0),
)


def iota(shape, dim):
    return lax.broadcasted_iota(I32, shape, dim)


def dot(a, b):
    return jnp.dot(a, b, preferred_element_type=F32)


def halves(x):
    hi = x.astype(BF16)
    return hi, (x - hi.astype(F32)).astype(BF16)


def prepare(
    ids, in_weight, in_bias, bucket_bias, norm_gain, mid_weight, mid_bias, head_gain,
    head_weight, head_bias, u, we, wb, cols, end,
):
    for a in range(3):
        for d in range(3):
            taps = [mid_weight[9 * a + 3 * b + d] for b in range(3)]
            outer, inner = taps[0] + taps[2], taps[1]
            s4 = taps[0] * (1 / 24) + taps[2] * (1 / 6)
            made = (
                taps[0] * 0.25,
                (outer + inner) * (-1 / 6),
                (inner - outer) * (1 / 6),
                s4 + inner * (1 / 12),
                s4 - inner * (1 / 12),
                taps[2],
            )
            for w in range(6):
                hi, lo = halves(made[w])
                rows = pl.ds((2 - a) * CH, CH)
                u[w, rows, pl.ds(d * CH, CH)] = hi
                u[w, rows, pl.ds((3 + d) * CH, CH)] = hi
                u[w, rows, pl.ds((6 + d) * CH, CH)] = lo
    n = iota((81, LANES), 1)
    d, part, h, m = n // 72, n % 72 // 24, n % 24 // 12, n % 12
    key = 3 * d + m % 3
    row = 2 * (m // 3) + h
    first = n < 216
    k = iota((81, LANES), 0)
    whi, wlo = halves(jnp.transpose(in_weight[...]))
    lines = jnp.concatenate(
        [in_bias[...], bucket_bias[...], norm_gain[...], mid_bias[...], head_gain[...]], axis=0
    )
    table = jnp.transpose(lines)
    lane = iota((CH, LANES), 1)
    offsets = jnp.zeros((CH, LANES), F32)
    for c in range(CLIPS):
        rest = table[:, 0:1] + sum(
            table[:, 1 + b : 2 + b] * jnp.where(ids[c] == b, 1.0, 0.0) for b in range(4)
        )
        for i in range(3):
            piece = rest.astype(BF16).astype(F32)
            offsets = jnp.where(lane == 216 + 3 * c + i, piece, offsets)
            rest = rest - piece
    for re in range(6):
        b = row - re
        legal = first & (b >= 0) & (b <= 2)
        for a in range(3):
            hit = legal & (k == 27 * a + 9 * b + key)
            e01 = jnp.where(hit & (part < 2), 1.0, 0.0).astype(BF16)
            e2 = jnp.where(hit & (part == 2), 1.0, 0.0).astype(BF16)
            got = dot(whi, e01) + dot(wlo, e2)
            if a == 2:
                got = got + offsets
            we[pl.ds(re * CH, CH), pl.ds(a * LANES, LANES)] = got.astype(BF16)
    for i, (at, scale) in enumerate(((5, 0.5), (6, 1.0), (7, 0.5))):
        cols[i] = jnp.broadcast_to(table[:, at : at + 1] * scale, (CH, 128))
    line = iota((128, ZCH), 0)
    spread = jnp.where(line % 64 // 4 == iota((128, ZCH), 1), 1.0, 0.0)
    hhi, hlo = halves(head_weight[...])
    line = iota((128, CH), 0)
    for part, piece in enumerate((hhi, hlo)):
        wide = dot(spread.astype(BF16), piece)
        for c4 in range(4):
            for r in range(2):
                q2, s = c4 // 2, c4 % 2
                keep = (line // 64 == q2) & (line % 2 == s) & (line % 4 // 2 == r)
                at = (c4 * 2 + r) * CH
                wb[pl.ds(part * 128, 128), pl.ds(at, CH)] = jnp.where(keep, wide, 0.0).astype(BF16)
    hb = jnp.sum(spread * head_bias[...], axis=1, keepdims=True)
    end[...] = jnp.broadcast_to(hb, (128, 128))


def exchange_kernel(
    loaded, tile_rows, bucket_ids, in_weight, in_bias, bucket_bias, norm_gain, mid_weight, mid_bias,
    head_gain, head_weight, head_bias,
    video, u, we, wb, cols, end,
    raw, numbers_smem, ids, weight_in, bias_in, buckets, gain1, weight_mid, bias_mid, gain2,
    weight_head, bias_head, in_sems,
    got, picked, sent, send1, recv1, send2, recv2, own_sem,
):
    o, g = lax.axis_index("dp"), lax.axis_index("seq")
    barrier = pltpu.get_barrier_semaphore()
    for k in FAR_SEQ:
        pl.semaphore_signal(barrier, 1, device_id=(o, lax.rem(g + k, 16)), device_id_type=MESH)
    for k in FAR_DP:
        pl.semaphore_signal(barrier, 1, device_id=(lax.rem(o + k, 16), g), device_id_type=MESH)
    sources = (
        loaded, tile_rows, bucket_ids, in_weight, in_bias, bucket_bias, norm_gain, mid_weight,
        mid_bias, head_gain, head_weight, head_bias,
    )
    targets = (
        raw, numbers_smem, ids, weight_in, bias_in, buckets, gain1, weight_mid, bias_mid, gain2,
        weight_head, bias_head,
    )
    loads = [
        pltpu.make_async_copy(a, b, in_sems.at[i]) for i, (a, b) in enumerate(zip(sources, targets))
    ]
    for load in loads:
        load.start()
    loads[0].wait()
    loads[1].wait()
    lane = iota((1, 128), 1)
    numbers = jnp.full((1, 128), -1000.0, F32)
    for j in range(6):
        numbers = jnp.where(lane == 8 * o + j, numbers_smem[0, j].astype(F32), numbers)
        for at, t in enumerate(PIECES):
            got[o, pl.ds(1 + 6 * at + j, 1), :] = raw[j, :, t * 128 : t * 128 + 128]
    got[o, 0:1, :] = numbers
    picked[:, 0:128] = jnp.zeros((16, 128), F32)
    picked[:, 128 + TILE :] = jnp.zeros((16, 128), F32)
    pl.semaphore_wait(barrier, 30)

    for c, (start, rows) in enumerate(CHUNKS):
        part = got.at[o, pl.ds(start, rows)]
        for k in range(1, 16):
            pltpu.make_async_remote_copy(
                src_ref=part,
                dst_ref=part,
                send_sem=send1,
                recv_sem=recv1.at[c],
                device_id=(lax.rem(o + k, 16), g),
                device_id_type=MESH,
            ).start()

    for load in loads[2:]:
        load.wait()
    prepare(
        ids, weight_in, bias_in, buckets, gain1, weight_mid, bias_mid, gain2, weight_head,
        bias_head, u, we, wb, cols, end,
    )

    lane = iota((16, 128), 1)
    hot2 = None
    done = 0
    for c, (start, rows) in enumerate(CHUNKS):
        wait_for(got.at[pl.ds(0, 15), pl.ds(start, rows)], recv1.at[c])
        if c == 0:
            label = got[0, 0:1, :]
            for l in range(1, 16):
                label = jnp.maximum(label, got[l, 0:1, :])
            m = iota((16, 128), 0)
            pg, colour = m // 3, m % 3
            wanted = 6 * o + 6 * ((pg + 1) // 2 - 1) + 2 * colour + (pg + 1) % 2
            hot = jnp.where((label == wanted.astype(F32)) & (m < 12), 1.0, 0.0).astype(BF16)
            hot2 = jnp.concatenate([hot, hot], axis=1)
        for at in range(max(start - 1, 0) // 6, (start + rows - 1) // 6):
            pieces = []
            for l in range(16):
                pieces += [got[l, pl.ds(1 + 6 * at, 6), :], jnp.zeros((2, 128), F32)]
            hi, lo = halves(jnp.concatenate(pieces, axis=0))
            column = 128 * (PIECES[at] + 1)
            picked[:, column : column + 128] = dot(hot2, jnp.concatenate([hi, lo], axis=0))
        count = WINDOWS[c]
        for s in range(done, done + count):
            col = lane % 64 + (COLS * s - 4)
            keep = (col >= 0) & (col < W)
            pieces = []
            for h in range(2):
                first = 128 + h * W + COLS * s - 4
                at = first // 128 * 128
                turned = pltpu.roll(picked[:, at : at + 256], (h * 64 - (first - at)) % 256, 1)
                pieces.append(turned[:, 0:128])
            both = jnp.where(lane < 64, pieces[0], pieces[1])
            sent[s] = jnp.where(keep, both, 0.0)
        for k in range(count):
            s = done + lax.rem(g + k, count)

            @pl.when(s != g)
            def _():
                pltpu.make_async_remote_copy(
                    src_ref=sent.at[s, pl.ds(0, 12)],
                    dst_ref=video.at[g, pl.ds(0, 12)],
                    send_sem=send2,
                    recv_sem=recv2,
                    device_id=(o, s),
                    device_id_type=MESH,
                ).start()

        done += count
    own = pltpu.make_async_copy(sent.at[g, pl.ds(0, 12)], video.at[g, pl.ds(0, 12)], own_sem)
    own.start()
    own.wait()
    wait_for(video.at[pl.ds(0, 15), pl.ds(0, 12)], recv2)


def wait_for(ref, sem):
    pltpu.make_async_copy(ref, ref, sem).wait()


def encode_kernel(
    position, video, u, we, wb, cols, end,
    out, x3, entry, xs, sums, mixed, zs, turned,
):
    o, s = position()
    lane = iota((1, LANES), 1)
    c4, t = lane // 64, lane % 16
    col = COLS * s + 4 * (t - 1) + c4
    in_frame = jnp.where((col >= 0) & (col < W), 1.0, 0.0)
    low = iota((16, 128), 1) < 64

    low12 = iota((12, 128), 1) < 64
    k = iota((LANES, LANES), 0)
    j = iota((LANES, LANES), 1)
    source = j % 64 // 16 * 64 + 4 * (j % 16) + j // 64
    permute = jnp.where(k == source, 1.0, 0.0).astype(BF16)
    which_clip = jnp.where(
        iota((40, LANES), 0) // 3 == iota((40, LANES), 1) % 64 // 16, 1.0, 0.0
    )

    def pixels_of(f):
        blocks = [video[4 * clip + f, 0:12, :] for clip in range(CLIPS)]
        flipped = [pltpu.roll(x, 64, 1) for x in blocks]
        first = [jnp.where(low12, blocks[c], flipped[c + 1]) for c in (0, 2)]
        second = [jnp.where(low12, flipped[c], blocks[c + 1]) for c in (0, 2)]
        wide = jnp.concatenate(
            [jnp.concatenate(first, axis=1), jnp.concatenate(second, axis=1)], axis=0
        )
        hi = wide.astype(BF16).astype(F32)
        block = dot(jnp.concatenate([hi, wide - hi], axis=0).astype(BF16), permute)
        v0, v1 = block[:, 0:128], block[:, 128:256]
        left, middle, right = shifted(v0, v1, iota((48, 128), 1) < 64)
        taps = []
        for a, b in ((left, middle), (v0, v1), (middle, right)):
            both = jnp.concatenate([a, b], axis=1)
            taps += [both, both[0:24]]
        taps.append(which_clip)
        x3[pl.ds(f * LANES, LANES), :] = jnp.concatenate(taps, axis=0).astype(BF16)

    def wide_column(which, at):
        column = cols[which, pl.ds(at, 16), :]
        return jnp.concatenate([column, column], axis=1)

    def shifted(v0, v1, select):
        b10, b32 = pltpu.roll(v0, 64, 1), pltpu.roll(v1, 64, 1)
        b3s, b0s = pltpu.roll(v1, 65, 1), pltpu.roll(v0, 63, 1)
        left = jnp.where(select, b3s, b10)
        middle = jnp.where(select, b10, b32)
        right = jnp.where(select, b32, b0s)
        return left, middle, right

    scales = {}

    def entry_dot(f):
        first = max(0, f - 2)
        k0 = (2 - (f - first)) * LANES
        entry[f] = dot(we[:, k0:], x3[pl.ds(first * LANES, (f - first + 1) * LANES), :])

    def entry_norm(f):
        inverse = []
        for re in range(6):
            total = jnp.zeros((8, LANES), F32)
            for c in range(0, CH, 8):
                value = entry[f, pl.ds(re * CH + c, 8), :]
                total = total + value * value
            mean = jnp.sum(total, axis=0, keepdims=True) * (1 / CH)
            scale = lax.rsqrt(mean + EPSILON) * in_frame
            if re == 0:
                scale = scale * jnp.where(o > 0, 1.0, 0.0)
            if re == 5:
                scale = scale * jnp.where(o < N_DP - 1, 1.0, 0.0)
            inverse.append(scale)
        scales[f] = inverse

    def active_of(f):
        def group(i):
            inverse = scales[f]
            at = i * 16
            gain = wide_column(0, at)
            act = []
            for re in range(6):
                v = entry[f, pl.ds(re * CH + at, 16), :] * inverse[re] * gain
                act.append(v + v * jnp.tanh(v))
            d0, d1, d2, d3, d4, d5 = act
            a, b = d4 - 4 * d2, d3 - 4 * d1
            c, e = d4 - d2, 2 * (d3 - d1)
            made = (4 * d0 - 5 * d2 + d4, a + b, a - b, c + e, c - e, 4 * d1 - 5 * d3 + d5)
            for w in range(6):
                v0, v1 = made[w][:, 0:128], made[w][:, 128:256]
                left, middle, right = shifted(v0, v1, low)
                his, los = zip(*[halves(x) for x in (left, middle, right, v0, v1)])
                for d, (p, q) in enumerate(((0, 1), (3, 4), (1, 2))):
                    for part, source in enumerate((his, los, his)):
                        rows = pl.ds((part * 3 + d) * CH + at, 16)
                        xs[f, w, rows, 0:128] = source[p]
                        xs[f, w, rows, 128:256] = source[q]

        return [functools.partial(group, i) for i in range(CH // 16)]

    def middle_of(f):
        reach = min(3, FRAMES - f)

        def step(w):
            y = dot(u[w, 0 : reach * CH, :], xs[f, w])
            for later in range(reach):
                part = y[later * CH : (later + 1) * CH]
                if f == 0 or later == 2:
                    sums[f + later, w] = part
                else:
                    sums[f + later, w] = sums[f + later, w] + part

        return [functools.partial(step, w) for w in range(6)]

    squares = {}

    def mixed_of(f):
        def group(i):
            at = i * 16
            bias = wide_column(1, at)
            y = [sums[f, w, pl.ds(at, 16), :] for w in range(6)]
            s12, d12, s34, d34 = y[1] + y[2], y[1] - y[2], y[3] + y[4], y[3] - y[4]
            made = (y[0] + s12 + s34, d12 + 2 * d34, s12 + 4 * s34, d12 + 8 * d34 + y[5])
            fresh = []
            for r in range(4):
                v = entry[f, pl.ds((r + 1) * CH + at, 16), :] + bias + made[r]
                mixed[f, r, pl.ds(at, 16), :] = v
                fresh.append(v * v + squares[f][r] if i else v * v)
            squares[f] = fresh

        return [functools.partial(group, i) for i in range(CH // 16)]

    def latent_of(f):
        side = pl.ds(f % 2 * 128, 128)

        def group(i):
            if i == 0:
                squares[f] = [
                    lax.rsqrt(jnp.sum(x, axis=0, keepdims=True) * (1 / CH) + EPSILON)
                    for x in squares[f]
                ]
            inverse = squares[f]
            at = i * 16
            gain = wide_column(2, at)
            act = []
            for r in range(4):
                v = mixed[f, r, pl.ds(at, 16), :] * inverse[r] * gain
                act.append(v + v * jnp.tanh(v))
            for r in range(2):
                for pair in range(2):
                    p0 = act[r][:, pair * 128 : pair * 128 + 128]
                    p1 = act[2 + r][:, pair * 128 : pair * 128 + 128]
                    even = jnp.where(low, p0, pltpu.roll(p1, 64, 1))
                    odd = jnp.where(low, pltpu.roll(p0, 64, 1), p1)
                    for c, x in ((2 * pair, even), (2 * pair + 1, odd)):
                        hi, lo = halves(x)
                        rows = pl.ds((c * 2 + r) * CH + at, 16)
                        zs[f // 2, 0, rows, side] = hi
                        zs[f // 2, 1, rows, side] = lo

        return [functools.partial(group, i) for i in range(CH // 16)]

    def tokens_of(first, count):
        lanes = pl.ds(first % 2 * 128, count * 128)
        part = [zs[first // 2, i, :, lanes] for i in range(2)]
        both = dot(wb[...], part[0])
        bias = jnp.concatenate([end[...]] * count, axis=1)
        made = both[0:128] + both[128:256] + dot(wb[0:128], part[1]) + bias
        turned[first // 2, lanes, :] = jnp.transpose(made)
        for f in range(first, first + count):
            for clip in range(CLIPS):
                for t in range(13):
                    rows = pl.ds(f % 2 * 128 + clip * 16 + t + 1, 2, stride=64)
                    out[clip * 4 + f, :, pl.ds(t * 128, 128)] = turned[first // 2, rows, :]

    def beside(main, *others):
        rest = [task for tasks in others for task in tasks]
        for i, task in enumerate(main):
            task()
            for other in rest[i * len(rest) // len(main) : (i + 1) * len(rest) // len(main)]:
                other()

    def run(f, task):
        return [functools.partial(task, f)]

    pixels_of(0)
    entry_dot(0)
    pixels_of(1)
    entry_dot(1)
    entry_norm(0)
    pixels_of(2)
    pixels_of(3)
    beside(active_of(0), run(2, entry_dot), run(3, entry_dot), run(1, entry_norm))
    beside(middle_of(0), active_of(1), run(2, entry_norm))
    beside(middle_of(1), active_of(2), mixed_of(0), latent_of(0), run(3, entry_norm))
    beside(middle_of(2), active_of(3), mixed_of(1), latent_of(1))
    beside(middle_of(3), mixed_of(2), latent_of(2), [functools.partial(tokens_of, 0, 2)])
    tokens_of(2, 1)
    for tasks in (mixed_of(3), latent_of(3)):
        for task in tasks:
            task()
    tokens_of(3, 1)


def shape(dims, dtype):
    return jax.ShapeDtypeStruct(dims, dtype)


MADE = (
    shape((6, 3 * CH, MID_K), BF16),
    shape((6 * CH, 3 * LANES), BF16),
    shape((256, 8 * CH), BF16),
    shape((3, CH, 128), F32),
    shape((128, 128), F32),
)
VMEM_BYTES = 48 * 2**20
VMEM = pl.BlockSpec(memory_space=pltpu.VMEM)
HBM = pl.BlockSpec(memory_space=pltpu.HBM)
ENCODE_SCRATCH = [
    pltpu.VMEM((FRAMES * LANES, LANES), BF16),
    pltpu.VMEM((FRAMES, 6 * CH, LANES), F32),
    pltpu.VMEM((FRAMES, 6, MID_K, LANES), BF16),
    pltpu.VMEM((FRAMES, 6, CH, LANES), F32),
    pltpu.VMEM((FRAMES, 4, CH, LANES), F32),
    pltpu.VMEM((2, 2, 8 * CH, LANES), BF16),
    pltpu.VMEM((2, LANES, 128), F32),
]


def whole_kernel(*refs):
    args, out, (made, exchange, encode) = refs[:12], refs[12], refs[13:]
    exchange_kernel(*args, *made, *exchange)
    encode_kernel(where_am_i, *made, out, *encode)
    got, _, sent, send1, _, send2 = exchange[13:19]
    wait_for(got.at[pl.ds(0, 15), pl.ds(0, 79)], send1)
    wait_for(sent.at[pl.ds(0, 15), pl.ds(0, 12)], send2)


def where_am_i():
    return lax.axis_index("dp"), lax.axis_index("seq")


def body(
    loaded, tile_rows, bucket_ids, in_weight, in_bias, bucket_bias, norm_gain, mid_weight,
    mid_bias, head_gain, head_weight, head_bias,
):
    def line(x):
        return x.reshape(1, -1)

    operands = (
        jnp.transpose(loaded, (1, 0, 2)), tile_rows, bucket_ids, in_weight.T, line(in_bias),
        bucket_bias, line(norm_gain), mid_weight, line(mid_bias), line(head_gain), head_weight,
        line(head_bias),
    )
    return pl.pallas_call(
        whole_kernel,
        out_shape=pltpu.VMEM((NF, 2, TILE), F32),
        in_specs=[HBM] * 12,
        out_specs=VMEM,
        scratch_shapes=[
            [pltpu.VMEM((NF, 16, 128), F32)] + [pltpu.VMEM(x.shape, x.dtype) for x in MADE],
            [
                pltpu.VMEM((6, 1, TILE), F32),
                pltpu.SMEM((1, 6), I32),
                pltpu.SMEM((4,), I32),
                pltpu.VMEM((81, CH), F32),
                pltpu.VMEM((1, CH), F32),
                pltpu.VMEM((4, CH), F32),
                pltpu.VMEM((1, CH), F32),
                pltpu.VMEM((27, CH, CH), F32),
                pltpu.VMEM((1, CH), F32),
                pltpu.VMEM((1, CH), F32),
                pltpu.VMEM((ZCH, CH), F32),
                pltpu.VMEM((1, ZCH), F32),
                pltpu.SemaphoreType.DMA((12,)),
                pltpu.VMEM((16, 80, 128), F32),
                pltpu.VMEM((16, TILE + 256), F32),
                pltpu.VMEM((N_SEQ, 16, 128), F32),
                pltpu.SemaphoreType.DMA,
                pltpu.SemaphoreType.DMA((3,)),
                pltpu.SemaphoreType.DMA,
                pltpu.SemaphoreType.DMA,
                pltpu.SemaphoreType.DMA,
            ],
            ENCODE_SCRATCH,
        ],
        compiler_params=pltpu.CompilerParams(
            collective_id=0, has_side_effects=True, vmem_limit_bytes=VMEM_BYTES
        ),
    )(*[pltpu.with_memory_space_constraint(x, pltpu.HBM) for x in operands])


def solution(mesh):
    return jax.shard_map(
        body,
        mesh=mesh,
        in_specs=(P("seq", "dp", None), P("seq", "dp")) + (P(),) * 10,
        out_specs=P(None, "dp", "seq"),
        check_vma=False,
    )
```

```python
import functools

import jax
import jax.numpy as jnp
from jax import lax
from jax.experimental import pallas as pl
from jax.experimental.pallas import tpu as pltpu
from jax.sharding import PartitionSpec as P

F32, BF16, I32 = jnp.float32, jnp.bfloat16, jnp.int32
MESH = pl.DeviceIdType.MESH
EPSILON = 1e-06
CH = 96
ZCH = 16
W = 832
NF = 16
FRAMES = 4
CLIPS = 4
N_DP = 16
N_SEQ = 16
COLS = W // N_SEQ
TILE = 2 * W
LANES = 256
MID_K = 9 * CH
PIECES = (0, 6, 7, 1, 8, 2, 9, 3, 10, 4, 11, 5, 12)
CHUNKS = ((0, 31), (31, 24), (55, 24))
WINDOWS = (4, 5, 7)
FAR_SEQ = (8, 9, 7, 6, 10, 5, 11, 4, 12, 3, 13, 2, 14, 1, 15)
FAR_DP = (10, 6, 9, 11, 14, 2, 8, 5, 7, 13, 15, 1, 3, 4, 12)


G43 = (
    (1 / 4, 0.0, 0.0),
    (-1 / 6, -1 / 6, -1 / 6),
    (-1 / 6, 1 / 6, -1 / 6),
    (1 / 24, 1 / 12, 1 / 6),
    (1 / 24, -1 / 12, 1 / 6),
    (0.0, 0.0, 1.0),
)


def iota(shape, dim):
    return lax.broadcasted_iota(I32, shape, dim)


def dot(a, b):
    return jnp.dot(a, b, preferred_element_type=F32)


def halves(x):
    hi = x.astype(BF16)
    return hi, (x - hi.astype(F32)).astype(BF16)


def prepare(
    ids, in_weight, in_bias, bucket_bias, norm_gain, mid_weight, mid_bias, head_gain,
    head_weight, head_bias, u, we, wb, cols, end,
):
    for a in range(3):
        for d in range(3):
            taps = [mid_weight[9 * a + 3 * b + d] for b in range(3)]
            outer, inner = taps[0] + taps[2], taps[1]
            s4 = taps[0] * (1 / 24) + taps[2] * (1 / 6)
            made = (
                taps[0] * 0.25,
                (outer + inner) * (-1 / 6),
                (inner - outer) * (1 / 6),
                s4 + inner * (1 / 12),
                s4 - inner * (1 / 12),
                taps[2],
            )
            for w in range(6):
                hi, lo = halves(made[w])
                rows = pl.ds((2 - a) * CH, CH)
                u[w, rows, pl.ds(d * CH, CH)] = hi
                u[w, rows, pl.ds((3 + d) * CH, CH)] = hi
                u[w, rows, pl.ds((6 + d) * CH, CH)] = lo
    n = iota((81, LANES), 1)
    d, part, h, m = n // 72, n % 72 // 24, n % 24 // 12, n % 12
    key = 3 * d + m % 3
    row = 2 * (m // 3) + h
    first = n < 216
    k = iota((81, LANES), 0)
    whi, wlo = halves(jnp.transpose(in_weight[...]))
    lines = jnp.concatenate(
        [in_bias[...], bucket_bias[...], norm_gain[...], mid_bias[...], head_gain[...]], axis=0
    )
    table = jnp.transpose(lines)
    lane = iota((CH, LANES), 1)
    offsets = jnp.zeros((CH, LANES), F32)
    for c in range(CLIPS):
        rest = table[:, 0:1] + sum(
            table[:, 1 + b : 2 + b] * jnp.where(ids[c] == b, 1.0, 0.0) for b in range(4)
        )
        for i in range(3):
            piece = rest.astype(BF16).astype(F32)
            offsets = jnp.where(lane == 216 + 3 * c + i, piece, offsets)
            rest = rest - piece
    for re in range(6):
        b = row - re
        legal = first & (b >= 0) & (b <= 2)
        for a in range(3):
            hit = legal & (k == 27 * a + 9 * b + key)
            e01 = jnp.where(hit & (part < 2), 1.0, 0.0).astype(BF16)
            e2 = jnp.where(hit & (part == 2), 1.0, 0.0).astype(BF16)
            got = dot(whi, e01) + dot(wlo, e2)
            if a == 2:
                got = got + offsets
            we[pl.ds(re * CH, CH), pl.ds(a * LANES, LANES)] = got.astype(BF16)
    for i, (at, scale) in enumerate(((5, 0.5), (6, 1.0), (7, 0.5))):
        cols[i] = jnp.broadcast_to(table[:, at : at + 1] * scale, (CH, 128))
    line = iota((128, ZCH), 0)
    spread = jnp.where(line % 64 // 4 == iota((128, ZCH), 1), 1.0, 0.0)
    hhi, hlo = halves(head_weight[...])
    line = iota((128, CH), 0)
    for part, piece in enumerate((hhi, hlo)):
        wide = dot(spread.astype(BF16), piece)
        for c4 in range(4):
            for r in range(2):
                q2, s = c4 // 2, c4 % 2
                keep = (line // 64 == q2) & (line % 2 == s) & (line % 4 // 2 == r)
                at = (c4 * 2 + r) * CH
                wb[pl.ds(part * 128, 128), pl.ds(at, CH)] = jnp.where(keep, wide, 0.0).astype(BF16)
    hb = jnp.sum(spread * head_bias[...], axis=1, keepdims=True)
    end[...] = jnp.broadcast_to(hb, (128, 128))


def exchange_kernel(
    loaded, tile_rows, bucket_ids, in_weight, in_bias, bucket_bias, norm_gain, mid_weight, mid_bias,
    head_gain, head_weight, head_bias,
    video, u, we, wb, cols, end,
    raw, numbers_smem, ids, weight_in, bias_in, buckets, gain1, weight_mid, bias_mid, gain2,
    weight_head, bias_head, in_sems,
    got, picked, sent, send1, recv1, send2, recv2, own_sem,
):
    o, g = lax.axis_index("dp"), lax.axis_index("seq")
    barrier = pltpu.get_barrier_semaphore()
    for k in FAR_SEQ:
        pl.semaphore_signal(barrier, 1, device_id=(o, lax.rem(g + k, 16)), device_id_type=MESH)
    for k in FAR_DP:
        pl.semaphore_signal(barrier, 1, device_id=(lax.rem(o + k, 16), g), device_id_type=MESH)
    sources = (
        loaded, tile_rows, bucket_ids, in_weight, in_bias, bucket_bias, norm_gain, mid_weight,
        mid_bias, head_gain, head_weight, head_bias,
    )
    targets = (
        raw, numbers_smem, ids, weight_in, bias_in, buckets, gain1, weight_mid, bias_mid, gain2,
        weight_head, bias_head,
    )
    loads = [
        pltpu.make_async_copy(a, b, in_sems.at[i]) for i, (a, b) in enumerate(zip(sources, targets))
    ]
    for load in loads:
        load.start()
    loads[0].wait()
    loads[1].wait()
    lane = iota((1, 128), 1)
    numbers = jnp.full((1, 128), -1000.0, F32)
    for j in range(6):
        numbers = jnp.where(lane == 8 * o + j, numbers_smem[0, j].astype(F32), numbers)
        for at, t in enumerate(PIECES):
            got[o, pl.ds(1 + 6 * at + j, 1), :] = raw[j, :, t * 128 : t * 128 + 128]
    got[o, 0:1, :] = numbers
    picked[:, 0:128] = jnp.zeros((16, 128), F32)
    picked[:, 128 + TILE :] = jnp.zeros((16, 128), F32)
    pl.semaphore_wait(barrier, 30)

    for c, (start, rows) in enumerate(CHUNKS):
        part = got.at[o, pl.ds(start, rows)]
        for k in range(1, 16):
            pltpu.make_async_remote_copy(
                src_ref=part,
                dst_ref=part,
                send_sem=send1,
                recv_sem=recv1.at[c],
                device_id=(lax.rem(o + k, 16), g),
                device_id_type=MESH,
            ).start()

    for load in loads[2:]:
        load.wait()
    prepare(
        ids, weight_in, bias_in, buckets, gain1, weight_mid, bias_mid, gain2, weight_head,
        bias_head, u, we, wb, cols, end,
    )

    lane = iota((16, 128), 1)
    hot2 = None
    done = 0
    for c, (start, rows) in enumerate(CHUNKS):
        wait_for(got.at[pl.ds(0, 15), pl.ds(start, rows)], recv1.at[c])
        if c == 0:
            label = got[0, 0:1, :]
            for l in range(1, 16):
                label = jnp.maximum(label, got[l, 0:1, :])
            m = iota((16, 128), 0)
            pg, colour = m // 3, m % 3
            wanted = 6 * o + 6 * ((pg + 1) // 2 - 1) + 2 * colour + (pg + 1) % 2
            hot = jnp.where((label == wanted.astype(F32)) & (m < 12), 1.0, 0.0).astype(BF16)
            hot2 = jnp.concatenate([hot, hot], axis=1)
        for at in range(max(start - 1, 0) // 6, (start + rows - 1) // 6):
            pieces = []
            for l in range(16):
                pieces += [got[l, pl.ds(1 + 6 * at, 6), :], jnp.zeros((2, 128), F32)]
            hi, lo = halves(jnp.concatenate(pieces, axis=0))
            column = 128 * (PIECES[at] + 1)
            picked[:, column : column + 128] = dot(hot2, jnp.concatenate([hi, lo], axis=0))
        count = WINDOWS[c]
        for s in range(done, done + count):
            col = lane % 64 + (COLS * s - 4)
            keep = (col >= 0) & (col < W)
            pieces = []
            for h in range(2):
                first = 128 + h * W + COLS * s - 4
                at = first // 128 * 128
                turned = pltpu.roll(picked[:, at : at + 256], (h * 64 - (first - at)) % 256, 1)
                pieces.append(turned[:, 0:128])
            both = jnp.where(lane < 64, pieces[0], pieces[1])
            sent[s] = jnp.where(keep, both, 0.0)
        for k in range(count):
            s = done + lax.rem(g + k, count)

            @pl.when(s != g)
            def _():
                pltpu.make_async_remote_copy(
                    src_ref=sent.at[s, pl.ds(0, 12)],
                    dst_ref=video.at[g, pl.ds(0, 12)],
                    send_sem=send2,
                    recv_sem=recv2,
                    device_id=(o, s),
                    device_id_type=MESH,
                ).start()

        done += count
    own = pltpu.make_async_copy(sent.at[g, pl.ds(0, 12)], video.at[g, pl.ds(0, 12)], own_sem)
    own.start()
    own.wait()
    wait_for(video.at[pl.ds(0, 15), pl.ds(0, 12)], recv2)


def wait_for(ref, sem):
    pltpu.make_async_copy(ref, ref, sem).wait()


def encode_kernel(
    position, video, u, we, wb, cols, end,
    out, x3, entry, xs, sums, mixed, zs, turned,
):
    o, s = position()
    lane = iota((1, LANES), 1)
    c4, t = lane // 64, lane % 16
    col = COLS * s + 4 * (t - 1) + c4
    in_frame = jnp.where((col >= 0) & (col < W), 1.0, 0.0)
    low = iota((16, 128), 1) < 64

    low12 = iota((12, 128), 1) < 64
    k = iota((LANES, LANES), 0)
    j = iota((LANES, LANES), 1)
    source = j % 64 // 16 * 64 + 4 * (j % 16) + j // 64
    permute = jnp.where(k == source, 1.0, 0.0).astype(BF16)
    which_clip = jnp.where(
        iota((40, LANES), 0) // 3 == iota((40, LANES), 1) % 64 // 16, 1.0, 0.0
    )

    def pixels_of(f):
        blocks = [video[4 * clip + f, 0:12, :] for clip in range(CLIPS)]
        flipped = [pltpu.roll(x, 64, 1) for x in blocks]
        first = [jnp.where(low12, blocks[c], flipped[c + 1]) for c in (0, 2)]
        second = [jnp.where(low12, flipped[c], blocks[c + 1]) for c in (0, 2)]
        wide = jnp.concatenate(
            [jnp.concatenate(first, axis=1), jnp.concatenate(second, axis=1)], axis=0
        )
        hi = wide.astype(BF16).astype(F32)
        block = dot(jnp.concatenate([hi, wide - hi], axis=0).astype(BF16), permute)
        v0, v1 = block[:, 0:128], block[:, 128:256]
        left, middle, right = shifted(v0, v1, iota((48, 128), 1) < 64)
        taps = []
        for a, b in ((left, middle), (v0, v1), (middle, right)):
            both = jnp.concatenate([a, b], axis=1)
            taps += [both, both[0:24]]
        taps.append(which_clip)
        x3[pl.ds(f * LANES, LANES), :] = jnp.concatenate(taps, axis=0).astype(BF16)

    def wide_column(which, at):
        column = cols[which, pl.ds(at, 16), :]
        return jnp.concatenate([column, column], axis=1)

    def shifted(v0, v1, select):
        b10, b32 = pltpu.roll(v0, 64, 1), pltpu.roll(v1, 64, 1)
        b3s, b0s = pltpu.roll(v1, 65, 1), pltpu.roll(v0, 63, 1)
        left = jnp.where(select, b3s, b10)
        middle = jnp.where(select, b10, b32)
        right = jnp.where(select, b32, b0s)
        return left, middle, right

    scales = {}

    def entry_dot(f):
        first = max(0, f - 2)
        k0 = (2 - (f - first)) * LANES
        entry[f] = dot(we[:, k0:], x3[pl.ds(first * LANES, (f - first + 1) * LANES), :])

    def entry_norm(f):
        inverse = []
        for re in range(6):
            total = jnp.zeros((8, LANES), F32)
            for c in range(0, CH, 8):
                value = entry[f, pl.ds(re * CH + c, 8), :]
                total = total + value * value
            mean = jnp.sum(total, axis=0, keepdims=True) * (1 / CH)
            scale = lax.rsqrt(mean + EPSILON) * in_frame
            if re == 0:
                scale = scale * jnp.where(o > 0, 1.0, 0.0)
            if re == 5:
                scale = scale * jnp.where(o < N_DP - 1, 1.0, 0.0)
            inverse.append(scale)
        scales[f] = inverse

    def active_of(f):
        def group(i):
            inverse = scales[f]
            at = i * 16
            gain = wide_column(0, at)
            act = []
            for re in range(6):
                v = entry[f, pl.ds(re * CH + at, 16), :] * inverse[re] * gain
                act.append(v + v * jnp.tanh(v))
            d0, d1, d2, d3, d4, d5 = act
            a, b = d4 - 4 * d2, d3 - 4 * d1
            c, e = d4 - d2, 2 * (d3 - d1)
            made = (4 * d0 - 5 * d2 + d4, a + b, a - b, c + e, c - e, 4 * d1 - 5 * d3 + d5)
            for w in range(6):
                v0, v1 = made[w][:, 0:128], made[w][:, 128:256]
                left, middle, right = shifted(v0, v1, low)
                his, los = zip(*[halves(x) for x in (left, middle, right, v0, v1)])
                for d, (p, q) in enumerate(((0, 1), (3, 4), (1, 2))):
                    for part, source in enumerate((his, los)):
                        rows = pl.ds((part * 3 + d) * CH + at, 16)
                        xs[f, w, rows, 0:128] = source[p]
                        xs[f, w, rows, 128:256] = source[q]

        return [functools.partial(group, i) for i in range(CH // 16)]

    def middle_of(f):
        reach = min(3, FRAMES - f)

        def step(w):
            both = jnp.concatenate([xs[f, w], xs[f, w, 0 : 3 * CH]], axis=0)
            y = dot(u[w, 0 : reach * CH, :], both)
            for later in range(reach):
                part = y[later * CH : (later + 1) * CH]
                if f == 0 or later == 2:
                    sums[f + later, w] = part
                else:
                    sums[f + later, w] = sums[f + later, w] + part

        return [functools.partial(step, w) for w in range(6)]

    squares = {}

    def mixed_of(f):
        def group(i):
            at = i * 16
            bias = wide_column(1, at)
            y = [sums[f, w, pl.ds(at, 16), :] for w in range(6)]
            s12, d12, s34, d34 = y[1] + y[2], y[1] - y[2], y[3] + y[4], y[3] - y[4]
            made = (y[0] + s12 + s34, d12 + 2 * d34, s12 + 4 * s34, d12 + 8 * d34 + y[5])
            fresh = []
            for r in range(4):
                v = entry[f, pl.ds((r + 1) * CH + at, 16), :] + bias + made[r]
                mixed[f, r, pl.ds(at, 16), :] = v
                fresh.append(v * v + squares[f][r] if i else v * v)
            squares[f] = fresh

        return [functools.partial(group, i) for i in range(CH // 16)]

    def latent_of(f):
        side = pl.ds(f % 2 * 128, 128)

        def group(i):
            if i == 0:
                squares[f] = [
                    lax.rsqrt(jnp.sum(x, axis=0, keepdims=True) * (1 / CH) + EPSILON)
                    for x in squares[f]
                ]
            inverse = squares[f]
            at = i * 16
            gain = wide_column(2, at)
            act = []
            for r in range(4):
                v = mixed[f, r, pl.ds(at, 16), :] * inverse[r] * gain
                act.append(v + v * jnp.tanh(v))
            for r in range(2):
                for pair in range(2):
                    p0 = act[r][:, pair * 128 : pair * 128 + 128]
                    p1 = act[2 + r][:, pair * 128 : pair * 128 + 128]
                    even = jnp.where(low, p0, pltpu.roll(p1, 64, 1))
                    odd = jnp.where(low, pltpu.roll(p0, 64, 1), p1)
                    for c, x in ((2 * pair, even), (2 * pair + 1, odd)):
                        hi, lo = halves(x)
                        rows = pl.ds((c * 2 + r) * CH + at, 16)
                        zs[f // 2, 0, rows, side] = hi
                        zs[f // 2, 1, rows, side] = lo

        return [functools.partial(group, i) for i in range(CH // 16)]

    def tokens_of(first, count):
        lanes = pl.ds(first % 2 * 128, count * 128)
        part = [zs[first // 2, i, :, lanes] for i in range(2)]
        both = dot(wb[...], part[0])
        bias = jnp.concatenate([end[...]] * count, axis=1)
        made = both[0:128] + both[128:256] + dot(wb[0:128], part[1]) + bias
        turned[first // 2, lanes, :] = jnp.transpose(made)
        for f in range(first, first + count):
            for clip in range(CLIPS):
                for t in range(13):
                    rows = pl.ds(f % 2 * 128 + clip * 16 + t + 1, 2, stride=64)
                    out[clip * 4 + f, :, pl.ds(t * 128, 128)] = turned[first // 2, rows, :]

    def beside(main, *others):
        rest = [task for tasks in others for task in tasks]
        for i, task in enumerate(main):
            task()
            for other in rest[i * len(rest) // len(main) : (i + 1) * len(rest) // len(main)]:
                other()

    def run(f, task):
        return [functools.partial(task, f)]

    pixels_of(0)
    entry_dot(0)
    pixels_of(1)
    entry_dot(1)
    entry_norm(0)
    pixels_of(2)
    pixels_of(3)
    beside(active_of(0), run(2, entry_dot), run(3, entry_dot), run(1, entry_norm))
    beside(middle_of(0), active_of(1), run(2, entry_norm))
    beside(middle_of(1), active_of(2), mixed_of(0), latent_of(0), run(3, entry_norm))
    beside(middle_of(2), active_of(3), mixed_of(1), latent_of(1))
    beside(middle_of(3), mixed_of(2), latent_of(2), [functools.partial(tokens_of, 0, 2)])
    tokens_of(2, 1)
    for tasks in (mixed_of(3), latent_of(3)):
        for task in tasks:
            task()
    tokens_of(3, 1)


def shape(dims, dtype):
    return jax.ShapeDtypeStruct(dims, dtype)


MADE = (
    shape((6, 3 * CH, MID_K), BF16),
    shape((6 * CH, 3 * LANES), BF16),
    shape((256, 8 * CH), BF16),
    shape((3, CH, 128), F32),
    shape((128, 128), F32),
)
VMEM_BYTES = 48 * 2**20
VMEM = pl.BlockSpec(memory_space=pltpu.VMEM)
HBM = pl.BlockSpec(memory_space=pltpu.HBM)
ENCODE_SCRATCH = [
    pltpu.VMEM((FRAMES * LANES, LANES), BF16),
    pltpu.VMEM((FRAMES, 6 * CH, LANES), F32),
    pltpu.VMEM((FRAMES, 6, 6 * CH, LANES), BF16),
    pltpu.VMEM((FRAMES, 6, CH, LANES), F32),
    pltpu.VMEM((FRAMES, 4, CH, LANES), F32),
    pltpu.VMEM((2, 2, 8 * CH, LANES), BF16),
    pltpu.VMEM((2, LANES, 128), F32),
]


def whole_kernel(*refs):
    args, out, (made, exchange, encode) = refs[:12], refs[12], refs[13:]
    exchange_kernel(*args, *made, *exchange)
    encode_kernel(where_am_i, *made, out, *encode)
    got, _, sent, send1, _, send2 = exchange[13:19]
    wait_for(got.at[pl.ds(0, 15), pl.ds(0, 79)], send1)
    wait_for(sent.at[pl.ds(0, 15), pl.ds(0, 12)], send2)


def where_am_i():
    return lax.axis_index("dp"), lax.axis_index("seq")


def body(
    loaded, tile_rows, bucket_ids, in_weight, in_bias, bucket_bias, norm_gain, mid_weight,
    mid_bias, head_gain, head_weight, head_bias,
):
    def line(x):
        return x.reshape(1, -1)

    operands = (
        jnp.transpose(loaded, (1, 0, 2)), tile_rows, bucket_ids, in_weight.T, line(in_bias),
        bucket_bias, line(norm_gain), mid_weight, line(mid_bias), line(head_gain), head_weight,
        line(head_bias),
    )
    return pl.pallas_call(
        whole_kernel,
        out_shape=pltpu.VMEM((NF, 2, TILE), F32),
        in_specs=[HBM] * 12,
        out_specs=VMEM,
        scratch_shapes=[
            [pltpu.VMEM((NF, 16, 128), F32)] + [pltpu.VMEM(x.shape, x.dtype) for x in MADE],
            [
                pltpu.VMEM((6, 1, TILE), F32),
                pltpu.SMEM((1, 6), I32),
                pltpu.SMEM((4,), I32),
                pltpu.VMEM((81, CH), F32),
                pltpu.VMEM((1, CH), F32),
                pltpu.VMEM((4, CH), F32),
                pltpu.VMEM((1, CH), F32),
                pltpu.VMEM((27, CH, CH), F32),
                pltpu.VMEM((1, CH), F32),
                pltpu.VMEM((1, CH), F32),
                pltpu.VMEM((ZCH, CH), F32),
                pltpu.VMEM((1, ZCH), F32),
                pltpu.SemaphoreType.DMA((12,)),
                pltpu.VMEM((16, 80, 128), F32),
                pltpu.VMEM((16, TILE + 256), F32),
                pltpu.VMEM((N_SEQ, 16, 128), F32),
                pltpu.SemaphoreType.DMA,
                pltpu.SemaphoreType.DMA((3,)),
                pltpu.SemaphoreType.DMA,
                pltpu.SemaphoreType.DMA,
                pltpu.SemaphoreType.DMA,
            ],
            ENCODE_SCRATCH,
        ],
        compiler_params=pltpu.CompilerParams(
            collective_id=0, has_side_effects=True, vmem_limit_bytes=VMEM_BYTES
        ),
    )(*[pltpu.with_memory_space_constraint(x, pltpu.HBM) for x in operands])


def solution(mesh):
    return jax.shard_map(
        body,
        mesh=mesh,
        in_specs=(P("seq", "dp", None), P("seq", "dp")) + (P(),) * 10,
        out_specs=P(None, "dp", "seq"),
        check_vma=False,
    )
```
